128 devices in a mesh: ctx: 16 (over y_hi, z, core), dp: 8 (over x, y_lo).
Axes of the slice: x: 4, y: 4 (y_hi: 2, y_lo: 2; y = y_hi * 2 + y_lo), z: 4, core: 2. Of those that a mesh axis runs over, the one named last changes fastest.
Arguments:
- queries: bfloat16 [8192, 24576], P('ctx', 'dp'), may hold values from -170 to 170, as said below
- latent_cache: bfloat16 [8192, 576], P(('ctx', 'dp')), may hold values from -6 to 6
- doc_ids: int32 [8192], P('ctx'), may hold values from 0 to 15, never falling along the last dimension, each value on 1 to 1024 neighbouring positions
- w_key: bfloat16 [512, 16384], P(None, 'dp'), may hold values from -0.25 to 0.25
- w_value: bfloat16 [512, 16384], P(None, 'dp'), may hold values from -0.25 to 0.25
Outputs:
- attended: bfloat16 [8192, 16384], P('ctx', 'dp')
The draws below stay inside these ranges and needn't reach their ends.
Inputs may be any that keep to these rules, and one draw needn't show every extreme that they name: doc_ids never fall along the sequence; every document holds 1 to 1024 consecutive tokens and some document holds exactly 1024. `queries`: finite values.
All inputs are finite; a program needn't handle non-finite values.
Results may differ from the reference program's by a relative error of at most 0.014.
Values may be sent and summed in bfloat16 or wider, within the bound.
A program may use at most 192 MiB of HBM per device.

```python
import math
import jax
import jax.numpy as jnp
import numpy as np
from jax import lax

HEADS = 128
LATENT = 512
ROPE = 64
POSITION_FREE = 128
VDIM = 128
TOK_DEV = 512
WINDOW = 3
TOKENS = 8192
DOCS = 16
MAXDOC = 1024


def draw_queries(key, part):
    key = jax.random.fold_in(key, 17)
    full_shape = (TOKENS, HEADS * (POSITION_FREE + ROPE))
    draws_base = jax.random.normal(key, full_shape, jnp.float32)
    return jnp.clip(draws_base, -6.0, 6.0).astype(jnp.bfloat16)


def steps_of(own_key, shape, shards, least, largest):
    level = 1.0
    for position, shards_of in shards:
        draws = jax.random.uniform(jax.random.fold_in(jax.random.fold_in(own_key, 6), position), (shards_of,), jnp.float32, least / len(shards), largest / len(shards))
        level = level * jnp.repeat(jnp.exp(draws), shape[position] // shards_of).reshape((-1,) + (1,) * (len(shape) - 1 - position))
    return level


def split_up(count, total, limit, lean):
    portions = [(1 << 20) // math.isqrt(standing ** lean) + 1 for standing in range(2, count + 1)]
    surplus, given = total - limit - (count - 1), [1] * (count - 1)
    while surplus > 0:
        free = [i for i in range(count - 1) if given[i] < limit]
        whole, remaining = sum([portions[i] for i in free]), surplus
        for i in free:
            more = min(limit - given[i], max(1, remaining * portions[i] // whole), surplus)
            given[i] = given[i] + more
            surplus = surplus - more
    return np.array([limit] + given)


def uneven(key, amount, total, bound, slope):
    if amount == 2:
        one = jax.random.randint(key, (), max(1, total - bound), min(bound, total - 1) + 1)
        return jnp.stack([one, total - one])
    lengths = jnp.asarray(split_up(amount, total, bound, slope), jnp.int32)
    twos = (amount - 1) // 2
    donor, taker = lengths[1:1 + 2 * twos:2], lengths[2:2 + 2 * twos:2]
    margin = jnp.minimum(donor - 1, bound - taker)
    moved = jax.random.randint(jax.random.fold_in(key, 1), (twos,), 0, 1 << 20) % (margin + 1)
    lengths = lengths.at[1:1 + 2 * twos:2].set(donor - moved).at[2:2 + 2 * twos:2].set(taker + moved)
    return lengths[jax.random.permutation(jax.random.fold_in(key, 2), amount)]


def scatter_about(rng, shape, width, bound, cuts=(), kind=jnp.bfloat16):
    array = width * jax.random.normal(rng, shape, jnp.float32)
    if cuts:
        array = array * steps_of(rng, shape, cuts, -0.22, 0.18)
    return jnp.clip(array, -bound, bound).astype(kind)


def setup_inputs(seed: int = 0) -> dict:
    key_list = jax.random.split(jax.random.key(seed), 6)
    return {
        "queries": draw_queries(jax.random.fold_in(key_list[5], 71), 0),
        "latent_cache": scatter_about(key_list[1], (TOKENS, LATENT + ROPE), 1.0, 6.0, ((0, 128),)),
        "doc_ids": jnp.searchsorted(jnp.cumsum(uneven(key_list[2], DOCS, TOKENS, MAXDOC, 1)), jnp.arange(TOKENS), side="right").astype(jnp.int32),
        "w_key": scatter_about(key_list[3], (LATENT, HEADS * POSITION_FREE), LATENT ** -0.5, 0.25, ((1, 8),)),
        "w_value": scatter_about(key_list[4], (LATENT, HEADS * VDIM), LATENT ** -0.5, 0.25, ((1, 8),)),
    }


NEG_FILL = -1e+30

def reference(queries, latent_cache, doc_ids, w_key, w_value):
    blocks = TOKENS // TOK_DEV
    score_scale = 1.0 / math.sqrt(POSITION_FREE + ROPE)
    latent = latent_cache[:, :LATENT]
    rope_keys = latent_cache[:, LATENT:]
    front_pad = (WINDOW - 1) * TOK_DEV
    positions = jnp.arange(TOKENS, dtype=jnp.int32)
    key_pos = jnp.arange(-front_pad, TOKENS, dtype=jnp.int32)
    key_seg = jnp.concatenate([jnp.full((front_pad,), -1, jnp.int32), doc_ids.astype(jnp.int32)])

    def windows(column_data):
        pieces = []
        for piece_index in range(WINDOW):
            low = piece_index * TOK_DEV
            taken = column_data[low:low + blocks * TOK_DEV]
            pieces.append(taken.reshape((blocks, TOK_DEV) + column_data.shape[1:]))
        return jnp.concatenate(pieces, axis=1)
    query_pos = positions.reshape(blocks, TOK_DEV)
    query_seg = doc_ids.astype(jnp.int32).reshape(blocks, TOK_DEV)
    win_pos = windows(key_pos)
    win_seg = windows(key_seg)
    visible = (win_seg[:, None, :] == query_seg[:, :, None]) & (win_pos[:, None, :] <= query_pos[:, :, None])
    rotary_window_keys = windows(jnp.concatenate([jnp.zeros((front_pad, ROPE), jnp.bfloat16), rope_keys], axis=0))
    rotary_window_keys = rotary_window_keys.astype(jnp.float32)

    def one_head(head_index):
        head_key = lax.dynamic_slice_in_dim(w_key, head_index * POSITION_FREE, POSITION_FREE, 1)
        head_value = lax.dynamic_slice_in_dim(w_value, head_index * VDIM, VDIM, 1)
        key_rows = jnp.dot(latent, head_key, preferred_element_type=jnp.float32).astype(jnp.bfloat16)
        value_rows = jnp.dot(latent, head_value, preferred_element_type=jnp.float32).astype(jnp.bfloat16)
        key_rows = lax.optimization_barrier(key_rows)
        value_rows = lax.optimization_barrier(value_rows)
        key_window_rows = windows(jnp.concatenate([jnp.zeros((front_pad, POSITION_FREE), jnp.bfloat16), key_rows], axis=0))
        value_window_rows = windows(jnp.concatenate([jnp.zeros((front_pad, VDIM), jnp.bfloat16), value_rows], axis=0))
        query_for_head = lax.dynamic_slice_in_dim(queries, head_index * (POSITION_FREE + ROPE), POSITION_FREE + ROPE, 1)
        query_for_head = query_for_head.reshape(blocks, TOK_DEV, POSITION_FREE + ROPE).astype(jnp.float32)
        logit_scores = jnp.einsum('fxy,fmy->fxm', query_for_head[..., :POSITION_FREE], key_window_rows.astype(jnp.float32))
        logit_scores = logit_scores + jnp.einsum('fxy,fmy->fxm', query_for_head[..., POSITION_FREE:], rotary_window_keys)
        logit_scores = logit_scores * score_scale
        logit_scores = jnp.where(visible, logit_scores, NEG_FILL)
        row_peak = lax.optimization_barrier(jnp.max(logit_scores, axis=2))
        raw_weights = jnp.where(visible, jnp.exp(logit_scores - row_peak[..., None]), 0.0)
        weight_sum = lax.optimization_barrier(jnp.sum(raw_weights, axis=2))
        softmax_weights = lax.optimization_barrier(raw_weights.astype(jnp.bfloat16))
        blended_output = jnp.einsum('fai,fiv->fav', softmax_weights.astype(jnp.float32), value_window_rows.astype(jnp.float32))
        blended_output = blended_output / weight_sum[..., None]
        return blended_output.reshape(TOKENS, VDIM).astype(jnp.bfloat16)
    heads_out = lax.map(one_head, jnp.arange(HEADS, dtype=jnp.int32))
    return jnp.transpose(heads_out, (1, 0, 2)).reshape(TOKENS, HEADS * VDIM)
```

```python
import functools
import math

import jax
import jax.numpy as jnp
from jax import lax
from jax.experimental import pallas as pl
from jax.experimental.pallas import tpu as pltpu
from jax.sharding import PartitionSpec as P

MESH = pl.DeviceIdType.MESH
SHARDS = 8


def gather_kernel(lat_ref, docs_ref, lat_out, docs_out, lat_s, docs_s, send, recv, relay_send, relay_recv, misc_send, misc_recv, out_sem):
    ctx, dp = lax.axis_index("ctx"), lax.axis_index("dp")
    x, y, core = dp // 2, dp % 2, ctx % 2
    right_x, left_x, far_x = (x + 1) % 4, (x + 3) % 4, (x + 2) % 4
    partner = (ctx, x * 2 + 1 - y)
    right, left = (ctx, right_x * 2 + y), (ctx, left_x * 2 + y)
    next1, next2 = ((ctx + 1) % 16, dp), ((ctx + 2) % 16, dp)
    prev1, prev2 = ((ctx + 15) % 16, dp), ((ctx + 14) % 16, dp)
    sibling = (ctx + 1 - 2 * core, dp)
    shard = [column * 2 + row for column in (x, left_x, right_x, far_x) for row in (y, 1 - y)]

    barrier = pltpu.get_barrier_semaphore()
    for peer in (partner, right, left, next1, next2, prev1, prev2):
        pl.semaphore_signal(barrier, inc=1, device_id=peer, device_id_type=MESH)
    pl.semaphore_wait(barrier, 7)

    def remote(src, dst, send_sem, recv_sem, peer):
        return pltpu.make_async_remote_copy(
            src_ref=src, dst_ref=dst, send_sem=send_sem, recv_sem=recv_sem, device_id=peer, device_id_type=MESH)

    def piece(w, k, half=None):
        block = lat_s.at[2 * w, shard[k]]
        return block if half is None else block.at[pl.ds(32 * half, 32)]

    def copy(w, slot, src, dst, peer):
        return remote(src, dst, send.at[w, slot], recv.at[w, slot], peer)

    def to_partner(w, src):
        return copy(w, 0, src, piece(w, 0), partner)

    def to_right(w, k, src):
        return copy(w, 1 + k, src, piece(w, k), right)

    def to_left(w, k, src):
        return copy(w, 3 + k, src, piece(w, k), left)

    def on_right(w, k):
        return copy(w, 5 + k, piece(w, 2 + k, 0), piece(w, 2 + k, 0), right)

    def on_left(w, k):
        return copy(w, 7 + k, piece(w, 4 + k, 1), piece(w, 4 + k, 1), left)

    def got(w, slot):
        k, half = [(1, None), (2, None), (3, None), (4, None), (5, None), (6, 0), (7, 0), (6, 1), (7, 1)][slot]
        place = piece(w, k, half)
        copy(w, slot, place, place, partner).wait_recv()

    def relay(k):
        src = lat_s.at[2 - 2 * core, shard[k]]
        return remote(src, lat_s.at[1, shard[k]], relay_send.at[k], relay_recv.at[k], sibling)

    def relay_if(w, k):
        @pl.when(core == 1 - w)
        def _():
            relay(k).start()

    zc = remote(lat_ref, lat_s.at[0, dp], misc_send.at[0], misc_recv.at[0], next2)
    d1 = remote(docs_ref, docs_s.at[1], misc_send.at[1], misc_recv.at[1], next1)
    d2 = remote(docs_ref, docs_s.at[0], misc_send.at[2], misc_recv.at[2], next2)
    mine = pltpu.make_async_copy(lat_ref, lat_s.at[2, dp], misc_send.at[3])
    docs_mine = pltpu.make_async_copy(docs_ref, docs_s.at[2], misc_send.at[4])
    started = []

    def go(c):
        c.start()
        started.append(c)

    go(zc)
    mine.start()
    docs_mine.start()
    go(to_partner(1, lat_ref))
    go(to_right(1, 0, lat_ref))
    go(to_left(1, 0, lat_ref))
    go(d1)
    go(d2)
    mine.wait()
    relay_if(1, 0)
    zc.wait_recv()
    go(to_partner(0, piece(0, 0)))
    go(to_right(0, 0, piece(0, 0)))
    go(to_left(0, 0, piece(0, 0)))
    relay_if(0, 0)
    for w in (1, 0):
        got(w, 0)
        go(to_right(w, 1, piece(w, 1)))
        go(to_left(w, 1, piece(w, 1)))
        relay_if(w, 1)
    for w in (1, 0):
        for k in range(2):
            got(w, 1 + k)
            go(on_right(w, k))
            relay_if(w, 2 + k)
            got(w, 3 + k)
            go(on_left(w, k))
            relay_if(w, 4 + k)
    for w in (1, 0):
        for k in range(2):
            got(w, 5 + k)
            got(w, 7 + k)
            relay_if(w, 6 + k)
    outs = [pltpu.make_async_copy(lat_s.at[2 * w], lat_out.at[2 * w], out_sem.at[w]) for w in range(2)]
    for o in outs:
        o.start()
    for k in range(8):
        place = lat_s.at[1, shard[k]]
        remote(place, place, relay_send.at[k], relay_recv.at[k], sibling).wait_recv()
    last = pltpu.make_async_copy(lat_s.at[1], lat_out.at[1], out_sem.at[2])
    last.start()
    docs_mine.wait()
    d1.wait_recv()
    d2.wait_recv()
    docs_out[...] = docs_s[...]
    for o in outs:
        o.wait()
    last.wait()
    for c in started:
        c.wait_send()
    for k in range(8):
        relay(k).wait_send()


def gather(latent, docs):
    return pl.pallas_call(
        gather_kernel,
        out_shape=(jax.ShapeDtypeStruct((3, SHARDS, 64, 576), jnp.bfloat16), jax.ShapeDtypeStruct((3, 4, 128), jnp.int32)),
        in_specs=[pl.BlockSpec(memory_space=pltpu.VMEM)] * 2,
        out_specs=(pl.BlockSpec(memory_space=pl.ANY), pl.BlockSpec(memory_space=pltpu.VMEM)),
        scratch_shapes=[
            pltpu.VMEM((3, SHARDS, 64, 576), jnp.bfloat16),
            pltpu.VMEM((3, 4, 128), jnp.int32),
            pltpu.SemaphoreType.DMA((2, 9)),
            pltpu.SemaphoreType.DMA((2, 9)),
            pltpu.SemaphoreType.DMA((8,)),
            pltpu.SemaphoreType.DMA((8,)),
            pltpu.SemaphoreType.DMA((5,)),
            pltpu.SemaphoreType.DMA((3,)),
            pltpu.SemaphoreType.DMA((3,)),
        ],
        compiler_params=pltpu.CompilerParams(collective_id=0, has_side_effects=True, vmem_limit_bytes=20 * 2**20),
    )(latent, docs)


BIG = 1e30
C = math.log2(math.e) / math.sqrt(192)
LOW, HIGH = 2.0 ** -60, 2.0 ** 100
T = 256
NT = (((1,), (1,)), ((), ()))

def build_tails(docs_ref, lat_ref, tail_ref, qtail_ref):
    lane = lax.broadcasted_iota(jnp.int32, (128, 128), 1)
    for g in range(12):
        b, r = divmod(g, 4)
        row = jnp.broadcast_to(docs_ref[b, r:r + 1, :], (128, 128))
        col = jnp.transpose(row.astype(jnp.float32)).astype(jnp.int32)
        rope = lat_ref[g * 128:(g + 1) * 128, 512:576].astype(jnp.float32)
        rope = jnp.concatenate([rope, jnp.zeros((128, 64), jnp.float32)], axis=1)
        other = (lane >= 64) & (lane < 80) & (col != lane - 64)
        tail_ref[g * 128:(g + 1) * 128, :] = jnp.where(other, -BIG, rope).astype(jnp.bfloat16)
        if b == 2:
            qtail_ref[r * 128:(r + 1) * 128, :] = (col == lane - 64).astype(jnp.float32).astype(jnp.bfloat16)

def kernel(HP, q_ref, docs_ref, lat_ref, wk_ref, wv_ref, o_ref, k_s, v_s, q_s, tail_s, qtail_s, rng_s):
    @pl.when(pl.program_id(0) == 0)
    def _():
        build_tails(docs_ref, lat_ref, tail_s, qtail_s)

    def doc_at(i):
        b, r = divmod(i, 512)
        r, l = divmod(r, 128)
        return docs_ref[b, r, l]

    firsts = []
    for qb in range(2):
        head_doc = doc_at(1024 + qb * T)
        lo = jnp.int32(4 + qb)
        for c in reversed(range(qb, 4 + qb)):
            lo = jnp.where(doc_at(c * T + T - 1) == head_doc, c, lo)
        firsts.append(lo)
    first = jnp.minimum(firsts[0], firsts[1])
    for c in range(6):
        @pl.when((c >= first))
        def _(c=c):
            rows = pl.ds(c * T, T)
            lat = lat_ref[rows, :512]
            k_s[rows, :] = (jnp.dot(lat, wk_ref[...], preferred_element_type=jnp.float32)).astype(jnp.bfloat16)
            v_s[rows, :] = jnp.dot(lat, wv_ref[...], preferred_element_type=jnp.float32).astype(jnp.bfloat16)

    half = lax.broadcasted_iota(jnp.int32, (512, 128), 1) < 64
    qtail = qtail_s[...]
    for p in range(HP // 2):
        o = p * 384
        q_s[2 * p, :, :128] = q_ref[:, o:o + 128]
        q_s[2 * p, :, 128:] = jnp.where(half, q_ref[:, o + 128:o + 256], qtail)
        q_s[2 * p + 1, :, :128] = q_ref[:, o + 192:o + 320]
        rope = jnp.concatenate([q_ref[:, o + 320:o + 384], qtail[:, 64:]], axis=1)
        q_s[2 * p + 1, :, 128:] = rope

    ones = jnp.ones((T, 128), jnp.bfloat16)
    causal = lax.broadcasted_iota(jnp.int32, (T, T), 1) <= lax.broadcasted_iota(jnp.int32, (T, T), 0)

    def score(h, qb, c, diag):
        rows = pl.ds(c * T, T)
        keys = jnp.concatenate([k_s[rows, h * 128:(h + 1) * 128], tail_s[rows, :]], axis=1)
        s = lax.dot_general(q_s[h, pl.ds(qb * T, T), :], keys, NT, preferred_element_type=jnp.float32)
        s = s * C
        return jnp.where(causal, s, -BIG) if diag else s

    def values(h, c):
        return jnp.concatenate([v_s[pl.ds(c * T, T), h * 128:(h + 1) * 128], ones], axis=1)

    for qb in range(2):
        for n in range(1, 6):
            @pl.when((firsts[qb] == 5 + qb - n))
            def _(qb=qb, n=n):
                for h in range(HP):
                    end = 4 + qb
                    acc = None
                    for c in range(end - n + 1, end + 1):
                        p = jnp.exp2(score(h, qb, c, c == end)).astype(jnp.bfloat16)
                        t = jnp.dot(p, values(h, c), preferred_element_type=jnp.float32)
                        acc = t if acc is None else acc + t
                    total = acc[:, 128:]
                    o_ref[qb * T:(qb + 1) * T, h * 128:(h + 1) * 128] = (acc[:, :128] / total).astype(jnp.bfloat16)
                    if h == 0 and qb == 0:
                        rng_s[0], rng_s[1] = total, total
                    else:
                        rng_s[0] = jnp.minimum(rng_s[0], total)
                        rng_s[1] = jnp.maximum(rng_s[1], total)

    inside = (jnp.min(rng_s[0]) >= LOW) & (jnp.max(rng_s[1]) <= HIGH)

    @pl.when(jnp.logical_not(inside))
    def _():
        for qb in range(2):
            end = 4 + qb
            for h in range(HP):
                def body(c, state):
                    peak, acc = state
                    s = score(h, qb, c, False)
                    s = jnp.where(causal | (c < end), s, -BIG)
                    new = jnp.maximum(peak, jnp.max(s, axis=1, keepdims=True))
                    p = jnp.exp2(s - new).astype(jnp.bfloat16)
                    acc = acc * jnp.exp2(peak - new) + jnp.dot(p, values(h, c), preferred_element_type=jnp.float32)
                    return new, acc
                _, acc = lax.fori_loop(firsts[qb], end + 1, body, (jnp.full((T, 1), -BIG, jnp.float32), jnp.zeros((T, 256), jnp.float32)))
                o_ref[qb * T:(qb + 1) * T, h * 128:(h + 1) * 128] = (acc[:, :128] / acc[:, 128:]).astype(jnp.bfloat16)

def attend(q, docs, lat, wk, wv, HP=2):
    H = wk.shape[1] // 128
    return pl.pallas_call(
        functools.partial(kernel, HP),
        out_shape=jax.ShapeDtypeStruct((512, H * 128), jnp.bfloat16),
        grid_spec=pltpu.PrefetchScalarGridSpec(
            num_scalar_prefetch=0,
            grid=(H // HP,),
            in_specs=[
                pl.BlockSpec((512, HP * 192), lambda i: (0, i)),
                pl.BlockSpec((3, 4, 128), lambda i: (0, 0, 0)),
                pl.BlockSpec((1536, 576), lambda i: (0, 0)),
                pl.BlockSpec((512, HP * 128), lambda i: (0, i)),
                pl.BlockSpec((512, HP * 128), lambda i: (0, i)),
            ],
            out_specs=pl.BlockSpec((512, HP * 128), lambda i: (0, i)),
            scratch_shapes=[
                pltpu.VMEM((1536, HP * 128), jnp.bfloat16),
                pltpu.VMEM((1536, HP * 128), jnp.bfloat16),
                pltpu.VMEM((HP, 512, 256), jnp.bfloat16),
                pltpu.VMEM((1536, 128), jnp.bfloat16),
                pltpu.VMEM((512, 128), jnp.bfloat16),
                pltpu.VMEM((2, T, 128), jnp.float32),
            ]),
        compiler_params=pltpu.CompilerParams(vmem_limit_bytes=50 * 2**20),
    )(q, docs, lat, wk, wv)


def on_device(queries, latent_cache, doc_ids, w_key, w_value):
    window, docs = gather(latent_cache, doc_ids.reshape(4, 128))
    return attend(queries, docs, window.reshape(1536, 576), w_key, w_value, 8)


def solution(mesh):
    placed = (P("ctx", "dp"), P(("ctx", "dp"), None), P("ctx"), P(None, "dp"), P(None, "dp"))
    return jax.shard_map(on_device, mesh=mesh, in_specs=placed, out_specs=P("ctx", "dp"), check_vma=False)
```

```python
import functools
import math

import jax
import jax.numpy as jnp
from jax import lax
from jax.experimental import pallas as pl
from jax.experimental.pallas import tpu as pltpu
from jax.sharding import PartitionSpec as P

MESH = pl.DeviceIdType.MESH
BF16, F32 = jnp.bfloat16, jnp.float32
HEADS = 16
GROUP = 4
T = 256
BIG = 1e30
SCALE = math.log2(math.e) / math.sqrt(192)
LOW, HIGH = 2.0 ** -60, 2.0 ** 100
NT = (((1,), (1,)), ((), ()))


def scores(query, keys):
    return lax.dot_general(query, keys, NT, preferred_element_type=F32) * SCALE


def with_ones(value):
    return jnp.concatenate([value, jnp.ones((value.shape[0], 128), BF16)], axis=1)


def expand(rows, weight):
    return jnp.dot(rows, weight, preferred_element_type=F32).astype(BF16)


def documents_down(row):
    return jnp.transpose(jnp.broadcast_to(row, (128, 128)).astype(F32)).astype(jnp.int32)


def key_tail(rope, row):
    lane = lax.broadcasted_iota(jnp.int32, (128, 128), 1)
    other = (lane >= 64) & (lane < 80) & (documents_down(row) != lane - 64)
    rope = jnp.concatenate([rope.astype(F32), jnp.zeros((128, 64), F32)], axis=1)
    return jnp.where(other, -BIG, rope).astype(BF16)


def query_tail(row):
    lane = lax.broadcasted_iota(jnp.int32, (128, 128), 1)
    return (documents_down(row) == lane - 64).astype(F32).astype(BF16)


def causal_mask():
    return lax.broadcasted_iota(jnp.int32, (T, T), 1) <= lax.broadcasted_iota(jnp.int32, (T, T), 0)


def gather_kernel(lat_ref, docs_ref, q_ref, wk_ref, wv_ref,
                  lat_s, docs_s, qp, wk_s, wv_s, acc_s,
                  q_s, k_s, v_s, tail_s, qtail_s,
                  send, recv, relay_send, relay_recv, misc_send, misc_recv, load_sem):
    ctx, dp = lax.axis_index("ctx"), lax.axis_index("dp")
    x, y, core = dp // 2, dp % 2, ctx % 2
    right_x, left_x, far_x = (x + 1) % 4, (x + 3) % 4, (x + 2) % 4
    partner = (ctx, x * 2 + 1 - y)
    right, left = (ctx, right_x * 2 + y), (ctx, left_x * 2 + y)
    next1, next2 = ((ctx + 1) % 16, dp), ((ctx + 2) % 16, dp)
    prev1, prev2 = ((ctx + 15) % 16, dp), ((ctx + 14) % 16, dp)
    sibling = (ctx + 1 - 2 * core, dp)
    shard = [column * 2 + row for column in (x, left_x, right_x, far_x) for row in (y, 1 - y)]

    barrier = pltpu.get_barrier_semaphore()
    for peer in (partner, right, left, next1, next2, prev1, prev2):
        pl.semaphore_signal(barrier, inc=1, device_id=peer, device_id_type=MESH)

    loads = [pltpu.make_async_copy(src, dst, load_sem.at[i]) for i, (src, dst) in enumerate((
        (lat_ref, lat_s.at[2, dp]), (docs_ref, docs_s.at[2]), (q_ref, q_s), (wk_ref, wk_s), (wv_ref, wv_s)))]
    for c in loads:
        c.start()
    pl.semaphore_wait(barrier, 7)

    def remote(src, dst, send_sem, recv_sem, peer):
        return pltpu.make_async_remote_copy(
            src_ref=src, dst_ref=dst, send_sem=send_sem, recv_sem=recv_sem, device_id=peer, device_id_type=MESH)

    def piece(w, k, half=None):
        block = lat_s.at[2 * w, shard[k]]
        return block if half is None else block.at[pl.ds(32 * half, 32)]

    brings = {
        1: [(1, None), (2, None), (3, None), (4, None), (5, None), (6, 0), (7, 0), (6, 1), (7, 1)],
        0: [(1, None), (2, None), (4, None), (6, 0), (6, 1), (3, None), (5, None), (7, None)],
    }
    started = []

    def go(w, slot, src, dst, peer):
        c = remote(src, dst, send.at[w, slot], recv.at[w, slot], peer)
        c.start()
        started.append(c)

    def got(w, slot):
        place = piece(w, *brings[w][slot])
        remote(place, place, send.at[w, slot], recv.at[w, slot], partner).wait_recv()

    def same(w, slot, k, peer, half=None):
        go(w, slot, piece(w, k, half), piece(w, k, half), peer)

    def relay(k):
        return remote(lat_s.at[2 - 2 * core, shard[k]], lat_s.at[1, shard[k]], relay_send.at[k], relay_recv.at[k], sibling)

    def relay_if(w, k):
        @pl.when(core == 1 - w)
        def _():
            relay(k).start()

    onward = remote(lat_ref, lat_s.at[0, dp], misc_send.at[0], misc_recv.at[0], next2)
    stay = pltpu.make_async_copy(lat_ref, lat_s.at[0, dp], misc_recv.at[3])
    d1 = remote(docs_ref, docs_s.at[1], misc_send.at[1], misc_recv.at[1], next1)
    d2 = remote(docs_ref, docs_s.at[0], misc_send.at[2], misc_recv.at[2], next2)

    go(1, 0, lat_ref, piece(1, 0), partner)
    go(1, 1, lat_ref, piece(1, 0), right)
    go(1, 3, lat_ref, piece(1, 0), left)

    @pl.when(ctx < 14)
    def _():
        onward.start()

    @pl.when(ctx < 2)
    def _():
        stay.start()

    d1.start()
    d2.start()
    loads[0].wait()
    relay_if(1, 0)

    got(1, 0)
    same(1, 2, 1, right)
    same(1, 4, 1, left)
    relay_if(1, 1)

    @pl.when(ctx >= 2)
    def _():
        onward.wait_recv()

    @pl.when(ctx < 2)
    def _():
        stay.wait()

    same(0, 1, 0, right)
    same(0, 2, 0, left)
    same(0, 0, 0, partner)
    relay_if(0, 0)

    loads[1].wait()
    for r in range(4):
        qtail_s[pl.ds(128 * r, 128), :] = query_tail(docs_s[2, r:r + 1, :])
    loads[2].wait()
    qtail = qtail_s[...]

    def prepare(p, carry):
        a, b, c = [q_s[:, pl.ds(pl.multiple_of(p * 384 + 128 * i, 128), 128)] for i in range(3)]
        qp[2 * p, :, :128] = a
        qp[2 * p, :, 128:] = jnp.concatenate([b[:, :64], qtail[:, 64:]], axis=1)
        qp[2 * p + 1, :, :128] = jnp.concatenate([b[:, 64:], c[:, :64]], axis=1)
        qp[2 * p + 1, :, 128:] = jnp.concatenate([c[:, 64:], qtail[:, 64:]], axis=1)
        return carry

    lax.fori_loop(0, HEADS // 2, prepare, 0)

    got(1, 1)
    same(1, 5, 2, right, 0)
    relay_if(1, 2)
    got(1, 3)
    same(1, 7, 4, left, 1)
    relay_if(1, 4)
    got(1, 2)
    same(1, 6, 3, right, 0)
    relay_if(1, 3)
    got(1, 4)
    same(1, 8, 5, left, 1)
    relay_if(1, 5)
    got(0, 1)
    same(0, 3, 2, right, 0)
    same(0, 5, 2, partner)
    relay_if(0, 2)
    got(0, 2)
    same(0, 4, 4, left, 1)
    same(0, 6, 4, partner)
    relay_if(0, 4)
    got(1, 5)
    got(1, 7)
    relay_if(1, 6)
    got(1, 6)
    got(1, 8)
    relay_if(1, 7)

    loads[3].wait()
    loads[4].wait()
    for r in range(4):
        rope = lat_s[2, 2 * r:2 * r + 2, :, 512:].reshape(128, 64)
        tail_s[pl.ds(128 * r, 128), :] = key_tail(rope, docs_s[2, r:r + 1, :])

    def own(g, carry):
        columns = pl.ds(pl.multiple_of(g * GROUP * 128, 128), GROUP * 128)
        latent = lat_s[2, :, :, :512].reshape(512, 512)
        k_s[...] = expand(latent, wk_s[:, columns])
        v_s[...] = expand(latent, wv_s[:, columns])
        causal = causal_mask()
        tail = tail_s[...]
        for h in range(GROUP):
            head = g * GROUP + h
            keys = jnp.concatenate([k_s[:, h * 128:(h + 1) * 128], tail], axis=1)
            value = with_ones(v_s[:, h * 128:(h + 1) * 128])
            for qb in range(2):
                s = scores(qp[head, pl.ds(qb * T, T), :], keys[:(qb + 1) * T])
                diagonal = jnp.where(causal, s[:, qb * T:], -BIG)
                s = diagonal if qb == 0 else jnp.concatenate([s[:, :T], diagonal], axis=1)
                weights = jnp.exp2(s).astype(BF16)
                acc_s[head, pl.ds(qb * T, T), :] = jnp.dot(weights, value[:(qb + 1) * T], preferred_element_type=F32)
        return carry

    lax.fori_loop(0, 1, own, 0)
    got(0, 3)
    got(0, 4)
    same(0, 7, 6, partner)
    relay_if(0, 6)
    got(0, 0)
    relay_if(0, 1)
    got(0, 5)
    relay_if(0, 3)
    got(0, 6)
    relay_if(0, 5)
    lax.fori_loop(1, 2, own, 0)
    got(0, 7)
    relay_if(0, 7)
    lax.fori_loop(2, HEADS // GROUP, own, 0)

    d1.wait_recv()
    d2.wait_recv()
    for k in range(8):
        place = lat_s.at[1, shard[k]]
        remote(place, place, relay_send.at[k], relay_recv.at[k], sibling).wait_recv()
    for c in started:
        c.wait_send()
    for k in range(8):
        relay(k).wait_send()
    d1.wait_send()
    d2.wait_send()

    @pl.when(ctx < 14)
    def _():
        onward.wait_send()


def gather(latent, docs, queries, w_key, w_value):
    vmem, hbm = pl.BlockSpec(memory_space=pltpu.VMEM), pl.BlockSpec(memory_space=pltpu.HBM)
    operands = [pltpu.with_memory_space_constraint(a, pltpu.HBM) for a in (latent, docs, queries, w_key, w_value)]
    return pl.pallas_call(
        gather_kernel,
        out_shape=(
            pltpu.VMEM((3, 8, 64, 576), BF16),
            pltpu.VMEM((3, 4, 128), jnp.int32),
            pltpu.VMEM((HEADS, 512, 256), BF16),
            pltpu.VMEM((512, 2048), BF16),
            pltpu.VMEM((512, 2048), BF16),
            pltpu.VMEM((HEADS, 512, 256), F32),
        ),
        in_specs=[hbm] * 5,
        out_specs=(vmem,) * 6,
        scratch_shapes=[
            pltpu.VMEM((512, 3072), BF16),
            pltpu.VMEM((512, GROUP * 128), BF16),
            pltpu.VMEM((512, GROUP * 128), BF16),
            pltpu.VMEM((512, 128), BF16),
            pltpu.VMEM((512, 128), BF16),
            pltpu.SemaphoreType.DMA((2, 9)),
            pltpu.SemaphoreType.DMA((2, 9)),
            pltpu.SemaphoreType.DMA((8,)),
            pltpu.SemaphoreType.DMA((8,)),
            pltpu.SemaphoreType.DMA((3,)),
            pltpu.SemaphoreType.DMA((4,)),
            pltpu.SemaphoreType.DMA((5,)),
        ],
        compiler_params=pltpu.CompilerParams(collective_id=0, has_side_effects=True, vmem_limit_bytes=20 * 2**20),
    )(*operands)


def earlier_kernel(lat_ref, docs_ref, qp, wk_ref, wv_ref, acc_ref, out_ref, o_s, k_s, v_s, tail_s, rng_s, out_sem):
    def document(row):
        b, rest = divmod(row, 512)
        return docs_ref[b, rest // 128, rest % 128]

    def first_chunk(block):
        lowest = jnp.int32(4)
        for c in reversed(range(block, 4)):
            lowest = jnp.where(document(c * T + T - 1) == document(1024 + block * T), c, lowest)
        return lowest

    first, both = first_chunk(0), first_chunk(1) < 4
    lat = lat_ref.reshape(24, 64, 576)

    def tails(start, end):
        for r in range(start, end):
            rope = lat[2 * r:2 * r + 2, :, 512:].reshape(128, 64)
            tail_s[pl.ds(128 * r, 128), :] = key_tail(rope, docs_ref[r // 4, r % 4:r % 4 + 1, :])

    rng_s[0] = jnp.ones((T, 128), F32)
    rng_s[1] = jnp.ones((T, 128), F32)

    def store(g, h, row, acc):
        total = acc[:, 128:]
        o_s[g, pl.ds(row, acc.shape[0]), h * 128:(h + 1) * 128] = (acc[:, :128] / total).astype(BF16)
        for t in range(acc.shape[0] // T):
            rng_s[0] = jnp.minimum(rng_s[0], total[t * T:(t + 1) * T])
            rng_s[1] = jnp.maximum(rng_s[1], total[t * T:(t + 1) * T])

    def write(g):
        return pltpu.make_async_copy(o_s.at[g], out_ref.at[:, pl.ds(pl.multiple_of(g * GROUP * 128, 128), GROUP * 128)], out_sem.at[g])

    def run(start, reach):
        count = 4 - start
        if count:
            tails(2 * start, 8)

        def step(g, carry):
            columns = pl.ds(pl.multiple_of(g * GROUP * 128, 128), GROUP * 128)
            if count:
                latent = lat[4 * start:16, :, :512].reshape(count * T, 512)
                k_s[pl.ds(0, count * T), :] = expand(latent, wk_ref[:, columns])
                v_s[pl.ds(0, count * T), :] = expand(latent, wv_ref[:, columns])
            for h in range(GROUP):
                head = g * GROUP + h
                acc = acc_ref[head, pl.ds(0, reach), :]
                for c in range(count):
                    rows = pl.ds(c * T, T)
                    keys = jnp.concatenate([k_s[rows, h * 128:(h + 1) * 128], tail_s[pl.ds((start + c) * T, T), :]], axis=1)
                    weights = jnp.exp2(scores(qp[head, pl.ds(0, reach), :], keys)).astype(BF16)
                    acc = acc + jnp.dot(weights, with_ones(v_s[rows, h * 128:(h + 1) * 128]), preferred_element_type=F32)
                store(g, h, 0, acc)
                if reach < 512:
                    store(g, h, reach, acc_ref[head, pl.ds(reach, 512 - reach), :])
            write(g).start()
            return carry

        lax.fori_loop(0, HEADS // GROUP, step, 0)

    for start in range(5):
        for reach in ((512,) if start == 4 else (256,) if start == 0 else (256, 512)):
            chosen = first == start
            if start < 4:
                chosen = chosen & (both if reach == 512 else jnp.logical_not(both))
            pl.when(chosen)(functools.partial(run, start, reach))
    for g in range(HEADS // GROUP):
        write(g).wait()

    inside = (jnp.min(rng_s[0]) >= LOW) & (jnp.max(rng_s[1]) <= HIGH)

    @pl.when(jnp.logical_not(inside))
    def _():
        tails(0, 12)

        def group(g, carry):
            columns = pl.ds(pl.multiple_of(g * GROUP * 128, 128), GROUP * 128)

            def widen(c, carry):
                latent = lat[pl.ds(c * 4, 4), :, :512].reshape(T, 512)
                rows = pl.ds(pl.multiple_of(c * T, T), T)
                k_s[rows, :] = expand(latent, wk_ref[:, columns])
                v_s[rows, :] = expand(latent, wv_ref[:, columns])
                return carry

            lax.fori_loop(first, 6, widen, 0)
            causal = causal_mask()
            for h in range(GROUP):
                for qb in range(2):
                    end = 4 + qb

                    def body(c, state):
                        peak, acc = state
                        rows = pl.ds(pl.multiple_of(c * T, T), T)
                        keys = jnp.concatenate([k_s[rows, h * 128:(h + 1) * 128], tail_s[rows, :]], axis=1)
                        s = scores(qp[g * GROUP + h, pl.ds(qb * T, T), :], keys)
                        s = jnp.where(causal | (c < end), s, -BIG)
                        new = jnp.maximum(peak, jnp.max(s, axis=1, keepdims=True))
                        weights = jnp.exp2(s - new).astype(BF16)
                        t = jnp.dot(weights, with_ones(v_s[rows, h * 128:(h + 1) * 128]), preferred_element_type=F32)
                        return new, acc * jnp.exp2(peak - new) + t

                    initial = (jnp.full((T, 1), -BIG, F32), jnp.zeros((T, 256), F32))
                    _, acc = lax.fori_loop(first, end + 1, body, initial)
                    o_s[g, pl.ds(qb * T, T), h * 128:(h + 1) * 128] = (acc[:, :128] / acc[:, 128:]).astype(BF16)
            write(g).start()
            write(g).wait()
            return carry

        lax.fori_loop(0, HEADS // GROUP, group, 0)


def earlier(lat, docs, qp, w_key, w_value, acc):
    vmem, hbm = pl.BlockSpec(memory_space=pltpu.VMEM), pl.BlockSpec(memory_space=pltpu.HBM)
    return pl.pallas_call(
        earlier_kernel,
        out_shape=jax.ShapeDtypeStruct((512, 2048), BF16),
        in_specs=[vmem] * 6,
        out_specs=hbm,
        scratch_shapes=[
            pltpu.VMEM((HEADS // GROUP, 512, GROUP * 128), BF16),
            pltpu.VMEM((1536, GROUP * 128), BF16),
            pltpu.VMEM((1536, GROUP * 128), BF16),
            pltpu.VMEM((1536, 128), BF16),
            pltpu.VMEM((2, T, 128), F32),
            pltpu.SemaphoreType.DMA((HEADS // GROUP,)),
        ],
        compiler_params=pltpu.CompilerParams(vmem_limit_bytes=20 * 2**20),
    )(lat, docs, qp, w_key, w_value, acc)


def on_device(queries, latent_cache, doc_ids, w_key, w_value):
    lat, docs, qp, wk, wv, acc = gather(latent_cache, doc_ids.reshape(4, 128), queries, w_key, w_value)
    return earlier(lat, docs, qp, wk, wv, acc)


def solution(mesh):
    placed = (P("ctx", "dp"), P(("ctx", "dp"), None), P("ctx"), P(None, "dp"), P(None, "dp"))
    return jax.shard_map(on_device, mesh=mesh, in_specs=placed, out_specs=P("ctx", "dp"), check_vma=False)
```

```python
import functools
import math

import jax
import jax.numpy as jnp
from jax import lax
from jax.experimental import pallas as pl
from jax.experimental.pallas import tpu as pltpu
from jax.sharding import PartitionSpec as P

MESH = pl.DeviceIdType.MESH
BF16, F32 = jnp.bfloat16, jnp.float32
HEADS = 16
GROUP = 4
T = 256
BIG = 1e30
SCALE = math.log2(math.e) / math.sqrt(192)
LOW, HIGH = 2.0 ** -60, 2.0 ** 100
NT = (((1,), (1,)), ((), ()))


def scores(query, keys):
    return lax.dot_general(query, keys, NT, preferred_element_type=F32) * SCALE


def with_ones(value):
    return jnp.concatenate([value, jnp.ones((value.shape[0], 128), BF16)], axis=1)


def expand(rows, weight):
    return jnp.dot(rows, weight, preferred_element_type=F32).astype(BF16)


def documents_down(row):
    return jnp.transpose(jnp.broadcast_to(row, (128, 128)).astype(F32)).astype(jnp.int32)


def key_tail(rope, row):
    lane = lax.broadcasted_iota(jnp.int32, (128, 128), 1)
    other = (lane >= 64) & (lane < 80) & (documents_down(row) != lane - 64)
    rope = jnp.concatenate([rope.astype(F32), jnp.zeros((128, 64), F32)], axis=1)
    return jnp.where(other, -BIG, rope).astype(BF16)


def query_tail(row):
    lane = lax.broadcasted_iota(jnp.int32, (128, 128), 1)
    return (documents_down(row) == lane - 64).astype(F32).astype(BF16)


def causal_mask():
    return lax.broadcasted_iota(jnp.int32, (T, T), 1) <= lax.broadcasted_iota(jnp.int32, (T, T), 0)


def rows_of(window, shards):
    return jnp.concatenate([window[k, :, 512 * j:512 * j + 512] for k in shards for j in range(2)], axis=0)


def rope_of(window, shards):
    packed = [window[k, :, 1024:] for k in shards]
    return jnp.concatenate([p[:, 64 * j:64 * j + 64] for p in packed for j in range(2)], axis=0)


def gather_kernel(lat_ref, docs_ref, q_ref, wk_ref, wv_ref,
                  win, docs_s, qp, wk_s, wv_s, acc_s,
                  lat_s, own_s, q_s, k_s, v_s, tail_s, qtail_s,
                  send, recv, relay_send, relay_recv, misc_send, misc_recv, load_sem):
    ctx, dp = lax.axis_index("ctx"), lax.axis_index("dp")
    x, y, core = dp // 2, dp % 2, ctx % 2
    right_x, left_x, far_x = (x + 1) % 4, (x + 3) % 4, (x + 2) % 4
    partner = (ctx, x * 2 + 1 - y)
    right, left = (ctx, right_x * 2 + y), (ctx, left_x * 2 + y)
    next1, next2 = ((ctx + 1) % 16, dp), ((ctx + 2) % 16, dp)
    prev1, prev2 = ((ctx + 15) % 16, dp), ((ctx + 14) % 16, dp)
    sibling = (ctx + 1 - 2 * core, dp)
    shard = [column * 2 + row for column in (x, left_x, right_x, far_x) for row in (y, 1 - y)]

    barrier = pltpu.get_barrier_semaphore()

    def greet(peer):
        pl.semaphore_signal(barrier, inc=1, device_id=peer, device_id_type=MESH)

    for peer in (partner, right, left):
        greet(peer)
    pl.when(ctx >= 1)(lambda: greet(prev1))
    pl.when(ctx >= 2)(lambda: greet(prev2))
    pl.when(core == 0)(lambda: greet(sibling))

    loads = [pltpu.make_async_copy(src, dst, load_sem.at[i]) for i, (src, dst) in enumerate((
        (lat_ref, lat_s), (docs_ref, docs_s.at[2]), (q_ref, q_s), (wk_ref, wk_s), (wv_ref, wv_s)))]
    for c in loads:
        c.start()

    def remote(src, dst, send_sem, recv_sem, peer):
        return pltpu.make_async_remote_copy(
            src_ref=src, dst_ref=dst, send_sem=send_sem, recv_sem=recv_sem, device_id=peer, device_id_type=MESH)

    def piece(w, k, half=None):
        block = win.at[2 * w, shard[k]]
        return block if half is None else block.at[pl.ds(16 * half, 16)]

    brings = [(1, None), (2, None), (3, None), (4, None), (5, None), (6, 0), (7, 0), (6, 1), (7, 1)]
    started = []

    def go(w, slot, src, dst, peer):
        c = remote(src, dst, send.at[w, slot], recv.at[w, slot], peer)
        c.start()
        started.append(c)

    def got(w, slot):
        place = piece(w, *brings[slot])
        remote(place, place, send.at[w, slot], recv.at[w, slot], partner).wait_recv()

    def pass_on(w, slot, k, peer, half=None):
        go(w, slot, piece(w, k, half), piece(w, k, half), peer)

    def relay(k):
        return remote(win.at[2 - 2 * core, shard[k]], win.at[1, shard[k]], relay_send.at[k], relay_recv.at[k], sibling)

    def relay_if(w, k):
        @pl.when(core == 1 - w)
        def _():
            relay(k).start()

    loads[0].wait()
    packed = jnp.concatenate(
        [lat_s[:32, :512], lat_s[32:, :512], lat_s[:32, 512:], lat_s[32:, 512:]], axis=1)
    own_s[...] = packed
    win[2, dp] = packed

    loads[1].wait()
    for r in range(4):
        qtail_s[pl.ds(128 * r, 128), :] = query_tail(docs_s[2, r:r + 1, :])

    @pl.when(ctx < 2)
    def _():
        docs_s[0] = jnp.full((4, 128), -1, jnp.int32)
        win[0, dp] = packed

    @pl.when(ctx < 1)
    def _():
        docs_s[1] = jnp.full((4, 128), -1, jnp.int32)

    onward = remote(own_s, win.at[0, dp], misc_send.at[0], misc_recv.at[0], next2)
    d1 = remote(docs_ref, docs_s.at[1], misc_send.at[1], misc_recv.at[1], next1)
    d2 = remote(docs_ref, docs_s.at[0], misc_send.at[2], misc_recv.at[2], next2)

    pl.semaphore_wait(barrier, 3 + jnp.where(ctx < 15, 1, 0) + jnp.where(ctx < 14, 1, 0) + core)

    go(1, 0, own_s, piece(1, 0), partner)
    go(1, 1, own_s, piece(1, 0), right)
    go(1, 3, own_s, piece(1, 0), left)

    @pl.when(ctx < 14)
    def _():
        onward.start()
        d2.start()

    @pl.when(ctx < 15)
    def _():
        d1.start()

    relay_if(1, 0)

    loads[2].wait()
    qtail = qtail_s[...]

    def prepare(p, carry):
        a, b, c = [q_s[:, pl.ds(pl.multiple_of(p * 384 + 128 * i, 128), 128)] for i in range(3)]
        qp[2 * p, :, :128] = a
        qp[2 * p, :, 128:] = jnp.concatenate([b[:, :64], qtail[:, 64:]], axis=1)
        qp[2 * p + 1, :, :128] = jnp.concatenate([b[:, 64:], c[:, :64]], axis=1)
        qp[2 * p + 1, :, 128:] = jnp.concatenate([c[:, 64:], qtail[:, 64:]], axis=1)
        return carry

    lax.fori_loop(0, HEADS // 2, prepare, 0)

    got(1, 0)
    pass_on(1, 2, 1, right)
    pass_on(1, 4, 1, left)
    relay_if(1, 1)
    got(1, 1)
    pass_on(1, 5, 2, right, 0)
    got(1, 3)
    pass_on(1, 7, 4, left, 1)
    relay_if(1, 2)
    relay_if(1, 4)

    @pl.when(ctx >= 2)
    def _():
        onward.wait_recv()

    pass_on(0, 0, 0, partner)
    relay_if(0, 0)

    loads[3].wait()
    loads[4].wait()

    def widen(kinds):
        latent = rows_of(win.at[2], [shard[k] for k in kinds])

        def some(g, carry):
            columns = pl.ds(pl.multiple_of(g * 512, 512), 512)
            for weight, out in ((wk_s, k_s), (wv_s, v_s)):
                wide = expand(latent, weight[:, columns])
                for i, k in enumerate(kinds):
                    out[pl.ds(pl.multiple_of(shard[k] * 64, 64), 64), columns] = wide[64 * i:64 * i + 64]
            return carry

        lax.fori_loop(0, 4, some, 0)

    widen((0, 1, 2, 4))

    got(1, 2)
    pass_on(1, 6, 3, right, 0)
    got(1, 4)
    pass_on(1, 8, 5, left, 1)
    pass_on(0, 1, 0, right)
    pass_on(0, 3, 0, left)
    relay_if(1, 3)
    relay_if(1, 5)
    got(0, 0)
    pass_on(0, 2, 1, right)
    pass_on(0, 4, 1, left)
    relay_if(0, 1)
    got(1, 5)
    got(1, 7)
    relay_if(1, 6)
    got(1, 6)
    got(1, 8)
    relay_if(1, 7)
    widen((3, 5, 6, 7))

    for r in range(4):
        tail_s[pl.ds(128 * r, 128), :] = key_tail(rope_of(win.at[2], (2 * r, 2 * r + 1)), docs_s[2, r:r + 1, :])

    def own(g, carry):
        causal = causal_mask()
        tail = tail_s[...]
        for h in range(GROUP):
            head = g * GROUP + h
            columns = pl.ds(pl.multiple_of(head * 128, 128), 128)
            keys = jnp.concatenate([k_s[:, columns], tail], axis=1)
            value = with_ones(v_s[:, columns])
            for qb in range(2):
                s = scores(qp[head, pl.ds(qb * T, T), :], keys[:(qb + 1) * T])
                diagonal = jnp.where(causal, s[:, qb * T:], -BIG)
                s = diagonal if qb == 0 else jnp.concatenate([s[:, :T], diagonal], axis=1)
                weights = jnp.exp2(s).astype(BF16)
                acc_s[head, pl.ds(qb * T, T), :] = jnp.dot(weights, value[:(qb + 1) * T], preferred_element_type=F32)
        return carry

    lax.fori_loop(0, 1, own, 0)
    got(0, 1)
    pass_on(0, 5, 2, right, 0)
    got(0, 3)
    pass_on(0, 7, 4, left, 1)
    relay_if(0, 2)
    relay_if(0, 4)
    lax.fori_loop(1, 2, own, 0)
    got(0, 2)
    pass_on(0, 6, 3, right, 0)
    got(0, 4)
    pass_on(0, 8, 5, left, 1)
    relay_if(0, 3)
    relay_if(0, 5)
    lax.fori_loop(2, 3, own, 0)
    got(0, 5)
    got(0, 7)
    relay_if(0, 6)
    got(0, 6)
    got(0, 8)
    relay_if(0, 7)
    lax.fori_loop(3, HEADS // GROUP, own, 0)

    @pl.when(ctx >= 1)
    def _():
        d1.wait_recv()

    @pl.when(ctx >= 2)
    def _():
        d2.wait_recv()

    for k in range(8):
        place = win.at[1, shard[k]]
        remote(place, place, relay_send.at[k], relay_recv.at[k], sibling).wait_recv()
    for c in started:
        c.wait_send()
    for k in range(8):
        relay(k).wait_send()

    @pl.when(ctx < 14)
    def _():
        onward.wait_send()
        d2.wait_send()

    @pl.when(ctx < 15)
    def _():
        d1.wait_send()


def gather(latent, docs, queries, w_key, w_value):
    vmem, hbm = pl.BlockSpec(memory_space=pltpu.VMEM), pl.BlockSpec(memory_space=pltpu.HBM)
    operands = [pltpu.with_memory_space_constraint(a, pltpu.HBM) for a in (latent, docs, queries, w_key, w_value)]
    return pl.pallas_call(
        gather_kernel,
        out_shape=(
            pltpu.VMEM((3, 8, 32, 1152), BF16),
            pltpu.VMEM((3, 4, 128), jnp.int32),
            pltpu.VMEM((HEADS, 512, 256), BF16),
            pltpu.VMEM((512, 2048), BF16),
            pltpu.VMEM((512, 2048), BF16),
            pltpu.VMEM((HEADS, 512, 256), F32),
        ),
        in_specs=[hbm] * 5,
        out_specs=(vmem,) * 6,
        scratch_shapes=[
            pltpu.VMEM((64, 576), BF16),
            pltpu.VMEM((32, 1152), BF16),
            pltpu.VMEM((512, 3072), BF16),
            pltpu.VMEM((512, HEADS * 128), BF16),
            pltpu.VMEM((512, HEADS * 128), BF16),
            pltpu.VMEM((512, 128), BF16),
            pltpu.VMEM((512, 128), BF16),
            pltpu.SemaphoreType.DMA((2, 9)),
            pltpu.SemaphoreType.DMA((2, 9)),
            pltpu.SemaphoreType.DMA((8,)),
            pltpu.SemaphoreType.DMA((8,)),
            pltpu.SemaphoreType.DMA((3,)),
            pltpu.SemaphoreType.DMA((3,)),
            pltpu.SemaphoreType.DMA((5,)),
        ],
        compiler_params=pltpu.CompilerParams(collective_id=0, has_side_effects=True, vmem_limit_bytes=20 * 2**20),
    )(*operands)


def earlier_kernel(win_ref, docs_ref, qp, wk_ref, wv_ref, acc_ref, out_ref, o_s, k_s, v_s, tail_s, rng_s, out_sem):
    def document(row):
        b, rest = divmod(row, 512)
        return docs_ref[b, rest // 128, rest % 128]

    def first_chunk(block):
        lowest = jnp.int32(4)
        for c in reversed(range(block, 4)):
            lowest = jnp.where(document(c * T + T - 1) == document(1024 + block * T), c, lowest)
        return lowest

    first, both = first_chunk(0), first_chunk(1) < 4
    window = win_ref.reshape(24, 32, 1152)

    def tails(start, end):
        for r in range(start, end):
            rope = rope_of(window, (2 * r, 2 * r + 1))
            tail_s[pl.ds(128 * r, 128), :] = key_tail(rope, docs_ref[r // 4, r % 4:r % 4 + 1, :])

    rng_s[0] = jnp.ones((T, 128), F32)
    rng_s[1] = jnp.ones((T, 128), F32)

    def store(g, h, row, acc):
        total = acc[:, 128:]
        o_s[g, pl.ds(row, acc.shape[0]), h * 128:(h + 1) * 128] = (acc[:, :128] / total).astype(BF16)
        for t in range(acc.shape[0] // T):
            rng_s[0] = jnp.minimum(rng_s[0], total[t * T:(t + 1) * T])
            rng_s[1] = jnp.maximum(rng_s[1], total[t * T:(t + 1) * T])

    def write(g):
        return pltpu.make_async_copy(o_s.at[g], out_ref.at[:, pl.ds(pl.multiple_of(g * GROUP * 128, 128), GROUP * 128)], out_sem.at[g])

    def run(start, reach):
        count = 4 - start
        if count:
            tails(2 * start, 8)

        def step(g, carry):
            columns = pl.ds(pl.multiple_of(g * GROUP * 128, 128), GROUP * 128)
            if count:
                latent = rows_of(window, range(4 * start, 16))
                k_s[pl.ds(0, count * T), :] = expand(latent, wk_ref[:, columns])
                v_s[pl.ds(0, count * T), :] = expand(latent, wv_ref[:, columns])
            for h in range(GROUP):
                head = g * GROUP + h
                acc = acc_ref[head, pl.ds(0, reach), :]
                for c in range(count):
                    rows = pl.ds(c * T, T)
                    keys = jnp.concatenate([k_s[rows, h * 128:(h + 1) * 128], tail_s[pl.ds((start + c) * T, T), :]], axis=1)
                    weights = jnp.exp2(scores(qp[head, pl.ds(0, reach), :], keys)).astype(BF16)
                    acc = acc + jnp.dot(weights, with_ones(v_s[rows, h * 128:(h + 1) * 128]), preferred_element_type=F32)
                store(g, h, 0, acc)
                if reach < 512:
                    store(g, h, reach, acc_ref[head, pl.ds(reach, 512 - reach), :])
            write(g).start()
            return carry

        lax.fori_loop(0, HEADS // GROUP, step, 0)

    for start in range(5):
        for reach in ((512,) if start == 4 else (256,) if start == 0 else (256, 512)):
            chosen = first == start
            if start < 4:
                chosen = chosen & (both if reach == 512 else jnp.logical_not(both))
            pl.when(chosen)(functools.partial(run, start, reach))
    for g in range(HEADS // GROUP):
        write(g).wait()

    inside = (jnp.min(rng_s[0]) >= LOW) & (jnp.max(rng_s[1]) <= HIGH)

    @pl.when(jnp.logical_not(inside))
    def _():
        tails(0, 12)

        def group(g, carry):
            columns = pl.ds(pl.multiple_of(g * GROUP * 128, 128), GROUP * 128)

            def widen(c, carry):
                latent = rows_of(window, [4 * c + i for i in range(4)])
                rows = pl.ds(pl.multiple_of(c * T, T), T)
                k_s[rows, :] = expand(latent, wk_ref[:, columns])
                v_s[rows, :] = expand(latent, wv_ref[:, columns])
                return carry

            lax.fori_loop(first, 6, widen, 0)
            causal = causal_mask()
            for h in range(GROUP):
                for qb in range(2):
                    end = 4 + qb

                    def body(c, state):
                        peak, acc = state
                        rows = pl.ds(pl.multiple_of(c * T, T), T)
                        keys = jnp.concatenate([k_s[rows, h * 128:(h + 1) * 128], tail_s[rows, :]], axis=1)
                        s = scores(qp[g * GROUP + h, pl.ds(qb * T, T), :], keys)
                        s = jnp.where(causal | (c < end), s, -BIG)
                        new = jnp.maximum(peak, jnp.max(s, axis=1, keepdims=True))
                        weights = jnp.exp2(s - new).astype(BF16)
                        t = jnp.dot(weights, with_ones(v_s[rows, h * 128:(h + 1) * 128]), preferred_element_type=F32)
                        return new, acc * jnp.exp2(peak - new) + t

                    initial = (jnp.full((T, 1), -BIG, F32), jnp.zeros((T, 256), F32))
                    _, acc = lax.fori_loop(first, end + 1, body, initial)
                    o_s[g, pl.ds(qb * T, T), h * 128:(h + 1) * 128] = (acc[:, :128] / acc[:, 128:]).astype(BF16)
            write(g).start()
            write(g).wait()
            return carry

        lax.fori_loop(0, HEADS // GROUP, group, 0)


def earlier(window, docs, qp, w_key, w_value, acc):
    vmem, hbm = pl.BlockSpec(memory_space=pltpu.VMEM), pl.BlockSpec(memory_space=pltpu.HBM)
    return pl.pallas_call(
        earlier_kernel,
        out_shape=jax.ShapeDtypeStruct((512, 2048), BF16),
        in_specs=[vmem] * 6,
        out_specs=hbm,
        scratch_shapes=[
            pltpu.VMEM((HEADS // GROUP, 512, GROUP * 128), BF16),
            pltpu.VMEM((1536, GROUP * 128), BF16),
            pltpu.VMEM((1536, GROUP * 128), BF16),
            pltpu.VMEM((1536, 128), BF16),
            pltpu.VMEM((2, T, 128), F32),
            pltpu.SemaphoreType.DMA((HEADS // GROUP,)),
        ],
        compiler_params=pltpu.CompilerParams(vmem_limit_bytes=20 * 2**20),
    )(window, docs, qp, w_key, w_value, acc)


def on_device(queries, latent_cache, doc_ids, w_key, w_value):
    window, docs, qp, wk, wv, acc = gather(latent_cache, doc_ids.reshape(4, 128), queries, w_key, w_value)
    return earlier(window, docs, qp, wk, wv, acc)


def solution(mesh):
    placed = (P("ctx", "dp"), P(("ctx", "dp"), None), P("ctx"), P(None, "dp"), P(None, "dp"))
    return jax.shard_map(on_device, mesh=mesh, in_specs=placed, out_specs=P("ctx", "dp"), check_vma=False)
```

```python
import functools
import math

import jax
import jax.numpy as jnp
from jax import lax
from jax.experimental import pallas as pl
from jax.experimental.pallas import tpu as pltpu
from jax.sharding import PartitionSpec as P

MESH = pl.DeviceIdType.MESH
BF16, F32 = jnp.bfloat16, jnp.float32
HEADS = 16
GROUP = 4
T = 256
BIG = 1e30
SCALE = math.log2(math.e) / math.sqrt(192)
LOW, HIGH = 2.0 ** -60, 2.0 ** 100
NT = (((1,), (1,)), ((), ()))


def scores(query, keys):
    return lax.dot_general(query, keys, NT, preferred_element_type=F32) * SCALE


def with_ones(value):
    return jnp.concatenate([value, jnp.ones((value.shape[0], 128), BF16)], axis=1)


def expand(rows, weight):
    return jnp.dot(rows, weight, preferred_element_type=F32).astype(BF16)


def documents_down(row):
    return jnp.transpose(jnp.broadcast_to(row, (128, 128)).astype(F32)).astype(jnp.int32)


def key_tail(rope, row):
    lane = lax.broadcasted_iota(jnp.int32, (128, 128), 1)
    other = (lane >= 64) & (lane < 80) & (documents_down(row) != lane - 64)
    rope = jnp.concatenate([rope.astype(F32), jnp.zeros((128, 64), F32)], axis=1)
    return jnp.where(other, -BIG, rope).astype(BF16)


def query_tail(row):
    lane = lax.broadcasted_iota(jnp.int32, (128, 128), 1)
    return (documents_down(row) == lane - 64).astype(F32).astype(BF16)


def causal_mask():
    return lax.broadcasted_iota(jnp.int32, (T, T), 1) <= lax.broadcasted_iota(jnp.int32, (T, T), 0)


def rows_of(window, shards):
    return jnp.concatenate([window[k, :, 512 * j:512 * j + 512] for k in shards for j in range(2)], axis=0)


def rope_of(window, shards):
    packed = [window[k, :, 1024:] for k in shards]
    return jnp.concatenate([p[:, 64 * j:64 * j + 64] for p in packed for j in range(2)], axis=0)


def gather_kernel(lat_ref, docs_ref, q_ref, wk_ref, wv_ref,
                  win, docs_s, qp, wk_s, wv_s, acc_s,
                  lat_s, own_s, q_s, k_s, v_s, tail_s, qtail_s,
                  send, recv, relay_send, relay_recv, misc_send, misc_recv, load_sem):
    ctx, dp = lax.axis_index("ctx"), lax.axis_index("dp")
    x, y, core = dp // 2, dp % 2, ctx % 2
    right_x, left_x, far_x = (x + 1) % 4, (x + 3) % 4, (x + 2) % 4
    next1, next2 = ((ctx + 1) % 16, dp), ((ctx + 2) % 16, dp)
    prev1, prev2 = ((ctx + 15) % 16, dp), ((ctx + 14) % 16, dp)
    sibling = (ctx + 1 - 2 * core, dp)
    peers = {
        "partner": (ctx, x * 2 + 1 - y), "right": (ctx, right_x * 2 + y), "left": (ctx, left_x * 2 + y),
        "far": (ctx, far_x * 2 + y), "next": next2}
    turn = ctx // 2 == 4
    before_turn = ctx // 2 == 3
    shard = [column * 2 + row for column in (x, left_x, right_x, far_x) for row in (y, 1 - y)]
    kind_there = {
        "partner": lambda k: k ^ 1, "right": lambda k: 2 + k, "left": lambda k: 4 + k, "far": lambda k: 6 + k,
        "next": lambda k: k}

    barrier = pltpu.get_barrier_semaphore()

    def greet(peer):
        pl.semaphore_signal(barrier, inc=1, device_id=peer, device_id_type=MESH)

    for name in ("partner", "right", "left", "far"):
        greet(peers[name])
    pl.when(ctx >= 1)(lambda: greet(prev1))
    pl.when(ctx >= 2)(lambda: greet(prev2))
    pl.when(core == 0)(lambda: greet(sibling))

    loads = [pltpu.make_async_copy(src, dst, load_sem.at[i]) for i, (src, dst) in enumerate((
        (lat_ref, lat_s), (docs_ref, docs_s.at[2]), (q_ref, q_s), (wk_ref, wk_s), (wv_ref, wv_s)))]
    for c in loads:
        c.start()

    def remote(src, dst, send_sem, recv_sem, peer):
        return pltpu.make_async_remote_copy(
            src_ref=src, dst_ref=dst, send_sem=send_sem, recv_sem=recv_sem, device_id=peer, device_id_type=MESH)

    def piece(w, k):
        return win.at[2 * w, shard[k]]

    started = []

    def give(w, k, where, condition=None):
        to = 0 if where == "next" else w
        src = own_s if (w, k) == (1, 0) else piece(w, k)
        c = remote(src, win.at[2 * to, shard[k]], send.at[len(started)], recv.at[to, kind_there[where](k)], peers[where])
        started.append((c, condition))
        if condition is None:
            c.start()
        else:
            pl.when(condition)(c.start)

    def got(w, k):
        remote(piece(w, k), piece(w, k), send.at[0], recv.at[w, k], sibling).wait_recv()

    def relay(k):
        return remote(win.at[2 - 2 * core, shard[k]], win.at[1, shard[k]], relay_send.at[k], relay_recv.at[k], sibling)

    def relay_if(w, k):
        pl.when(core == 1 - w)(lambda: relay(k).start())

    loads[0].wait()
    packed = jnp.concatenate(
        [lat_s[:32, :512], lat_s[32:, :512], lat_s[:32, 512:], lat_s[32:, 512:]], axis=1)
    own_s[...] = packed
    win[2, dp] = packed

    loads[1].wait()
    for r in range(4):
        qtail_s[pl.ds(128 * r, 128), :] = query_tail(docs_s[2, r:r + 1, :])

    @pl.when(ctx < 2)
    def _():
        docs_s[0] = jnp.full((4, 128), -1, jnp.int32)
        for k in (0, 2, 4, 6):
            win[0, shard[k]] = packed

    @pl.when(ctx < 1)
    def _():
        docs_s[1] = jnp.full((4, 128), -1, jnp.int32)

    d1 = remote(docs_ref, docs_s.at[1], misc_send.at[0], misc_recv.at[0], next1)
    d2 = remote(docs_ref, docs_s.at[0], misc_send.at[1], misc_recv.at[1], next2)

    pl.semaphore_wait(barrier, 4 + jnp.where(ctx < 15, 1, 0) + jnp.where(ctx < 14, 1, 0) + core)

    for where in ("partner", "right", "left", "far"):
        give(1, 0, where)
    give(1, 0, "next", ctx < 14)
    pl.when(ctx < 14)(d2.start)
    pl.when(ctx < 15)(d1.start)
    relay_if(1, 0)

    loads[2].wait()
    qtail = qtail_s[...]

    def prepare(p, carry):
        a, b, c = [q_s[:, pl.ds(pl.multiple_of(p * 384 + 128 * i, 128), 128)] for i in range(3)]
        qp[2 * p, :, :128] = a
        qp[2 * p, :, 128:] = jnp.concatenate([b[:, :64], qtail[:, 64:]], axis=1)
        qp[2 * p + 1, :, :128] = jnp.concatenate([b[:, 64:], c[:, :64]], axis=1)
        qp[2 * p + 1, :, 128:] = jnp.concatenate([c[:, 64:], qtail[:, 64:]], axis=1)
        return carry

    lax.fori_loop(0, HEADS // 2, prepare, 0)

    def widen(kinds):
        latent = rows_of(win.at[2], [shard[k] for k in kinds])

        def some(g, carry):
            columns = pl.ds(pl.multiple_of(g * 512, 512), 512)
            for weight, out in ((wk_s, k_s), (wv_s, v_s)):
                wide = expand(latent, weight[:, columns])
                for i, k in enumerate(kinds):
                    out[pl.ds(pl.multiple_of(shard[k] * 64, 64), 64), columns] = wide[64 * i:64 * i + 64]
            return carry

        lax.fori_loop(0, 4, some, 0)

    def own(g, carry):
        causal = causal_mask()
        tail = tail_s[...]
        for h in range(GROUP):
            head = g * GROUP + h
            columns = pl.ds(pl.multiple_of(head * 128, 128), 128)
            keys = jnp.concatenate([k_s[:, columns], tail], axis=1)
            value = with_ones(v_s[:, columns])
            for qb in range(2):
                s = scores(qp[head, pl.ds(qb * T, T), :], keys[:(qb + 1) * T])
                diagonal = jnp.where(causal, s[:, qb * T:], -BIG)
                s = diagonal if qb == 0 else jnp.concatenate([s[:, :T], diagonal], axis=1)
                weights = jnp.exp2(s).astype(BF16)
                acc_s[head, pl.ds(qb * T, T), :] = jnp.dot(weights, value[:(qb + 1) * T], preferred_element_type=F32)
        return carry

    def owns(g):
        lax.fori_loop(g, g + 1, own, 0)

    forward = (ctx < 14) & jnp.logical_not(before_turn)

    def earlier_shard(k):
        pl.when(ctx >= 2)(lambda: got(0, k))
        c = remote(piece(0, k), piece(0, k), send.at[40 + k], recv.at[0, k ^ 1], peers["partner"])
        c.start()
        relay_if(0, k)

    def in_time(k):
        pl.when(jnp.logical_not(turn))(lambda: earlier_shard(k))

    def late(k):
        pl.when(turn)(lambda: earlier_shard(k))

    got(1, 1)
    for where in ("right", "left", "far"):
        give(1, 1, where)
    relay_if(1, 1)
    got(1, 2)
    give(1, 2, "next", forward)
    got(1, 4)
    give(1, 4, "next", forward)
    relay_if(1, 2)
    relay_if(1, 4)
    in_time(0)
    loads[3].wait()
    loads[4].wait()
    widen((0, 1, 2, 4))
    late(0)
    for where in ("right", "left", "far"):
        give(0, 0, where, turn)
    got(1, 6)
    give(1, 6, "next", forward)
    relay_if(1, 6)
    in_time(2)
    got(1, 3)
    relay_if(1, 3)
    got(1, 5)
    relay_if(1, 5)
    in_time(4)
    got(1, 7)
    relay_if(1, 7)
    widen((3, 5, 6, 7))
    for r in range(4):
        tail_s[pl.ds(128 * r, 128), :] = key_tail(rope_of(win.at[2], (2 * r, 2 * r + 1)), docs_s[2, r:r + 1, :])
    late(2)
    late(4)
    owns(0)
    earlier_shard(6)
    owns(1)
    for k in (1, 3):
        got(0, k)
        relay_if(0, k)
    owns(2)
    for k in (5, 7):
        got(0, k)
        relay_if(0, k)
    owns(3)

    pl.when(ctx >= 1)(d1.wait_recv)
    pl.when(ctx >= 2)(d2.wait_recv)
    for k in range(8):
        place = win.at[1, shard[k]]
        remote(place, place, relay_send.at[k], relay_recv.at[k], sibling).wait_recv()
    for c, condition in started:
        if condition is None:
            c.wait_send()
        else:
            pl.when(condition)(c.wait_send)
    for k in (0, 2, 4, 6):
        remote(piece(0, k), piece(0, k), send.at[40 + k], recv.at[0, k ^ 1], peers["partner"]).wait_send()
    for k in range(8):
        relay(k).wait_send()
    pl.when(ctx < 14)(d2.wait_send)
    pl.when(ctx < 15)(d1.wait_send)


def gather(latent, docs, queries, w_key, w_value):
    vmem, hbm = pl.BlockSpec(memory_space=pltpu.VMEM), pl.BlockSpec(memory_space=pltpu.HBM)
    operands = [pltpu.with_memory_space_constraint(a, pltpu.HBM) for a in (latent, docs, queries, w_key, w_value)]
    return pl.pallas_call(
        gather_kernel,
        out_shape=(
            pltpu.VMEM((3, 8, 32, 1152), BF16),
            pltpu.VMEM((3, 4, 128), jnp.int32),
            pltpu.VMEM((HEADS, 512, 256), BF16),
            pltpu.VMEM((512, 2048), BF16),
            pltpu.VMEM((512, 2048), BF16),
            pltpu.VMEM((HEADS, 512, 256), F32),
        ),
        in_specs=[hbm] * 5,
        out_specs=(vmem,) * 6,
        scratch_shapes=[
            pltpu.VMEM((64, 576), BF16),
            pltpu.VMEM((32, 1152), BF16),
            pltpu.VMEM((512, 3072), BF16),
            pltpu.VMEM((512, HEADS * 128), BF16),
            pltpu.VMEM((512, HEADS * 128), BF16),
            pltpu.VMEM((512, 128), BF16),
            pltpu.VMEM((512, 128), BF16),
            pltpu.SemaphoreType.DMA((48,)),
            pltpu.SemaphoreType.DMA((2, 8)),
            pltpu.SemaphoreType.DMA((8,)),
            pltpu.SemaphoreType.DMA((8,)),
            pltpu.SemaphoreType.DMA((2,)),
            pltpu.SemaphoreType.DMA((2,)),
            pltpu.SemaphoreType.DMA((5,)),
        ],
        compiler_params=pltpu.CompilerParams(collective_id=0, has_side_effects=True, vmem_limit_bytes=20 * 2**20),
    )(*operands)


def earlier_kernel(win_ref, docs_ref, qp, wk_ref, wv_ref, acc_ref, out_ref, o_s, k_s, v_s, tail_s, rng_s, out_sem):
    def document(row):
        b, rest = divmod(row, 512)
        return docs_ref[b, rest // 128, rest % 128]

    def first_chunk(block):
        lowest = jnp.int32(4)
        for c in reversed(range(block, 4)):
            lowest = jnp.where(document(c * T + T - 1) == document(1024 + block * T), c, lowest)
        return lowest

    first, both = first_chunk(0), first_chunk(1) < 4
    window = win_ref.reshape(24, 32, 1152)

    def tails(start, end):
        for r in range(start, end):
            rope = rope_of(window, (2 * r, 2 * r + 1))
            tail_s[pl.ds(128 * r, 128), :] = key_tail(rope, docs_ref[r // 4, r % 4:r % 4 + 1, :])

    rng_s[0] = jnp.ones((T, 128), F32)
    rng_s[1] = jnp.ones((T, 128), F32)

    def store(g, h, row, acc):
        total = acc[:, 128:]
        o_s[g, pl.ds(row, acc.shape[0]), h * 128:(h + 1) * 128] = (acc[:, :128] / total).astype(BF16)
        for t in range(acc.shape[0] // T):
            rng_s[0] = jnp.minimum(rng_s[0], total[t * T:(t + 1) * T])
            rng_s[1] = jnp.maximum(rng_s[1], total[t * T:(t + 1) * T])

    def write(g):
        return pltpu.make_async_copy(o_s.at[g], out_ref.at[:, pl.ds(pl.multiple_of(g * GROUP * 128, 128), GROUP * 128)], out_sem.at[g])

    def run(start, reach):
        count = 4 - start
        if count:
            tails(2 * start, 8)

        def step(g, carry):
            columns = pl.ds(pl.multiple_of(g * GROUP * 128, 128), GROUP * 128)
            if count:
                latent = rows_of(window, range(4 * start, 16))
                k_s[pl.ds(0, count * T), :] = expand(latent, wk_ref[:, columns])
                v_s[pl.ds(0, count * T), :] = expand(latent, wv_ref[:, columns])
            for h in range(GROUP):
                head = g * GROUP + h
                acc = acc_ref[head, pl.ds(0, reach), :]
                for c in range(count):
                    rows = pl.ds(c * T, T)
                    keys = jnp.concatenate([k_s[rows, h * 128:(h + 1) * 128], tail_s[pl.ds((start + c) * T, T), :]], axis=1)
                    weights = jnp.exp2(scores(qp[head, pl.ds(0, reach), :], keys)).astype(BF16)
                    acc = acc + jnp.dot(weights, with_ones(v_s[rows, h * 128:(h + 1) * 128]), preferred_element_type=F32)
                store(g, h, 0, acc)
                if reach < 512:
                    store(g, h, reach, acc_ref[head, pl.ds(reach, 512 - reach), :])
            write(g).start()
            return carry

        lax.fori_loop(0, HEADS // GROUP, step, 0)

    for start in range(5):
        for reach in ((512,) if start == 4 else (256,) if start == 0 else (256, 512)):
            chosen = first == start
            if start < 4:
                chosen = chosen & (both if reach == 512 else jnp.logical_not(both))
            pl.when(chosen)(functools.partial(run, start, reach))
    for g in range(HEADS // GROUP):
        write(g).wait()

    inside = (jnp.min(rng_s[0]) >= LOW) & (jnp.max(rng_s[1]) <= HIGH)

    @pl.when(jnp.logical_not(inside))
    def _():
        tails(0, 12)

        def group(g, carry):
            columns = pl.ds(pl.multiple_of(g * GROUP * 128, 128), GROUP * 128)

            def widen(c, carry):
                latent = rows_of(window, [4 * c + i for i in range(4)])
                rows = pl.ds(pl.multiple_of(c * T, T), T)
                k_s[rows, :] = expand(latent, wk_ref[:, columns])
                v_s[rows, :] = expand(latent, wv_ref[:, columns])
                return carry

            lax.fori_loop(first, 6, widen, 0)
            causal = causal_mask()
            for h in range(GROUP):
                for qb in range(2):
                    end = 4 + qb

                    def body(c, state):
                        peak, acc = state
                        rows = pl.ds(pl.multiple_of(c * T, T), T)
                        keys = jnp.concatenate([k_s[rows, h * 128:(h + 1) * 128], tail_s[rows, :]], axis=1)
                        s = scores(qp[g * GROUP + h, pl.ds(qb * T, T), :], keys)
                        s = jnp.where(causal | (c < end), s, -BIG)
                        new = jnp.maximum(peak, jnp.max(s, axis=1, keepdims=True))
                        weights = jnp.exp2(s - new).astype(BF16)
                        t = jnp.dot(weights, with_ones(v_s[rows, h * 128:(h + 1) * 128]), preferred_element_type=F32)
                        return new, acc * jnp.exp2(peak - new) + t

                    initial = (jnp.full((T, 1), -BIG, F32), jnp.zeros((T, 256), F32))
                    _, acc = lax.fori_loop(first, end + 1, body, initial)
                    o_s[g, pl.ds(qb * T, T), h * 128:(h + 1) * 128] = (acc[:, :128] / acc[:, 128:]).astype(BF16)
            write(g).start()
            write(g).wait()
            return carry

        lax.fori_loop(0, HEADS // GROUP, group, 0)


def earlier(window, docs, qp, w_key, w_value, acc):
    vmem, hbm = pl.BlockSpec(memory_space=pltpu.VMEM), pl.BlockSpec(memory_space=pltpu.HBM)
    return pl.pallas_call(
        earlier_kernel,
        out_shape=jax.ShapeDtypeStruct((512, 2048), BF16),
        in_specs=[vmem] * 6,
        out_specs=hbm,
        scratch_shapes=[
            pltpu.VMEM((HEADS // GROUP, 512, GROUP * 128), BF16),
            pltpu.VMEM((1536, GROUP * 128), BF16),
            pltpu.VMEM((1536, GROUP * 128), BF16),
            pltpu.VMEM((1536, 128), BF16),
            pltpu.VMEM((2, T, 128), F32),
            pltpu.SemaphoreType.DMA((HEADS // GROUP,)),
        ],
        compiler_params=pltpu.CompilerParams(vmem_limit_bytes=20 * 2**20),
    )(window, docs, qp, w_key, w_value, acc)


def on_device(queries, latent_cache, doc_ids, w_key, w_value):
    window, docs, qp, wk, wv, acc = gather(latent_cache, doc_ids.reshape(4, 128), queries, w_key, w_value)
    return earlier(window, docs, qp, wk, wv, acc)


def solution(mesh):
    placed = (P("ctx", "dp"), P(("ctx", "dp"), None), P("ctx"), P(None, "dp"), P(None, "dp"))
    return jax.shard_map(on_device, mesh=mesh, in_specs=placed, out_specs=P("ctx", "dp"), check_vma=False)
```

```python
import functools
import math

import jax
import jax.numpy as jnp
from jax import lax
from jax.experimental import pallas as pl
from jax.experimental.pallas import tpu as pltpu
from jax.sharding import PartitionSpec as P

MESH = pl.DeviceIdType.MESH
BF16, F32 = jnp.bfloat16, jnp.float32
HEADS = 16
UNROLLED = ((1, 512), (0, 256))
SOME = 2
T = 256
BIG = 1e30
SCALE = math.log2(math.e) / math.sqrt(192)
LOW, HIGH = 2.0 ** -60, 2.0 ** 100
NT = (((1,), (1,)), ((), ()))


def scores(query, keys):
    return lax.dot_general(query, keys, NT, preferred_element_type=F32) * SCALE


def with_ones(value):
    return jnp.concatenate([value, jnp.ones((value.shape[0], 128), BF16)], axis=1)


def expand(rows, weight):
    return jnp.dot(rows, weight, preferred_element_type=F32).astype(BF16)


def documents_down(row):
    return jnp.transpose(jnp.broadcast_to(row, (128, 128)).astype(F32)).astype(jnp.int32)


def document_mask(row):
    lane = lax.broadcasted_iota(jnp.int32, (128, 128), 1)
    other = (lane >= 64) & (lane < 80) & (documents_down(row) != lane - 64)
    return jnp.where(other, -BIG, 0.0).astype(BF16)


def key_tail(rope, mask):
    return jnp.concatenate([rope, mask[:, 64:]], axis=1)


def query_tail(row):
    lane = lax.broadcasted_iota(jnp.int32, (128, 128), 1)
    return (documents_down(row) == lane - 64).astype(F32).astype(BF16)


def causal_mask():
    return lax.broadcasted_iota(jnp.int32, (T, T), 1) <= lax.broadcasted_iota(jnp.int32, (T, T), 0)


def rows_of(window, shards):
    return jnp.concatenate([window[k, :, 512 * j:512 * j + 512] for k in shards for j in range(2)], axis=0)


def rope_of(window, shards):
    packed = [window[k, :, 1024:] for k in shards]
    return jnp.concatenate([p[:, 64 * j:64 * j + 64] for p in packed for j in range(2)], axis=0)


def gather_kernel(lat_ref, docs_ref, q_ref, wk_ref, wv_ref,
                  win, docs_s, qp, wk_s, wv_s, acc_s,
                  lat_s, own_s, q_s, k_s, v_s, tail_s, qtail_s, mask_s, causal_s,
                  send, recv, relay_send, relay_recv, misc_send, misc_recv, load_sem):
    ctx, dp = lax.axis_index("ctx"), lax.axis_index("dp")
    x, y, core = dp // 2, dp % 2, ctx % 2
    right_x, left_x, far_x = (x + 1) % 4, (x + 3) % 4, (x + 2) % 4
    next1, next2 = ((ctx + 1) % 16, dp), ((ctx + 2) % 16, dp)
    prev1, prev2 = ((ctx + 15) % 16, dp), ((ctx + 14) % 16, dp)
    sibling = (ctx + 1 - 2 * core, dp)
    peers = {
        "partner": (ctx, x * 2 + 1 - y), "right": (ctx, right_x * 2 + y), "left": (ctx, left_x * 2 + y),
        "far": (ctx, far_x * 2 + y), "next": next2}
    turn = ctx // 2 == 4
    before_turn = ctx // 2 == 3
    shard = [column * 2 + row for column in (x, left_x, right_x, far_x) for row in (y, 1 - y)]
    kind_there = {
        "partner": lambda k: k ^ 1, "right": lambda k: 2 + k, "left": lambda k: 4 + k, "far": lambda k: 6 + k,
        "next": lambda k: k}

    barrier = pltpu.get_barrier_semaphore()

    def greet(peer):
        pl.semaphore_signal(barrier, inc=1, device_id=peer, device_id_type=MESH)

    for name in ("partner", "right", "left", "far"):
        greet(peers[name])
    pl.when(ctx >= 1)(lambda: greet(prev1))
    pl.when(ctx >= 2)(lambda: greet(prev2))
    pl.when(core == 0)(lambda: greet(sibling))

    loads = [pltpu.make_async_copy(src, dst, load_sem.at[i]) for i, (src, dst) in enumerate((
        (lat_ref, lat_s), (docs_ref, docs_s.at[2]), (q_ref, q_s), (wk_ref, wk_s), (wv_ref, wv_s)))]
    for c in loads:
        c.start()

    def remote(src, dst, send_sem, recv_sem, peer):
        return pltpu.make_async_remote_copy(
            src_ref=src, dst_ref=dst, send_sem=send_sem, recv_sem=recv_sem, device_id=peer, device_id_type=MESH)

    def piece(w, k):
        return win.at[2 * w, shard[k]]

    started = []

    def give(w, k, where, condition=None):
        to = 0 if where == "next" else w
        src = own_s if (w, k) == (1, 0) else piece(w, k)
        c = remote(src, win.at[2 * to, shard[k]], send.at[len(started)], recv.at[to, kind_there[where](k)], peers[where])
        started.append((c, condition))
        if condition is None:
            c.start()
        else:
            pl.when(condition)(c.start)

    def got(w, k):
        remote(piece(w, k), piece(w, k), send.at[0], recv.at[w, k], sibling).wait_recv()

    def relay(k):
        return remote(win.at[2 - 2 * core, shard[k]], win.at[1, shard[k]], relay_send.at[k], relay_recv.at[k], sibling)

    def relay_if(w, k):
        pl.when(core == 1 - w)(lambda: relay(k).start())

    loads[0].wait()
    packed = jnp.concatenate(
        [lat_s[:32, :512], lat_s[32:, :512], lat_s[:32, 512:], lat_s[32:, 512:]], axis=1)
    own_s[...] = packed
    win[2, dp] = packed

    loads[1].wait()
    for r in range(4):
        qtail_s[pl.ds(128 * r, 128), :] = query_tail(docs_s[2, r:r + 1, :])
        mask_s[pl.ds(128 * r, 128), :] = document_mask(docs_s[2, r:r + 1, :])

    @pl.when(ctx < 2)
    def _():
        docs_s[0] = jnp.full((4, 128), -1, jnp.int32)
        for k in (0, 2, 4, 6):
            win[0, shard[k]] = packed

    @pl.when(ctx < 1)
    def _():
        docs_s[1] = jnp.full((4, 128), -1, jnp.int32)

    d1 = remote(docs_ref, docs_s.at[1], misc_send.at[0], misc_recv.at[0], next1)
    d2 = remote(docs_ref, docs_s.at[0], misc_send.at[1], misc_recv.at[1], next2)

    pl.semaphore_wait(barrier, 4 + jnp.where(ctx < 15, 1, 0) + jnp.where(ctx < 14, 1, 0) + core)

    for where in ("partner", "right", "left", "far"):
        give(1, 0, where)
    give(1, 0, "next", ctx < 14)
    pl.when(ctx < 14)(d2.start)
    pl.when(ctx < 15)(d1.start)
    relay_if(1, 0)

    loads[2].wait()
    qtail = qtail_s[...]

    def prepare(p, carry):
        a, b, c = [q_s[:, pl.ds(pl.multiple_of(p * 384 + 128 * i, 128), 128)] for i in range(3)]
        qp[2 * p, :, :128] = a
        qp[2 * p, :, 128:] = jnp.concatenate([b[:, :64], qtail[:, 64:]], axis=1)
        qp[2 * p + 1, :, :128] = jnp.concatenate([b[:, 64:], c[:, :64]], axis=1)
        qp[2 * p + 1, :, 128:] = jnp.concatenate([c[:, 64:], qtail[:, 64:]], axis=1)
        return carry

    lax.fori_loop(0, HEADS // 2, prepare, 0)

    sets = ((0, 1, 2, 4), (3, 5, 6, 7))

    def widen(i):
        latent = rows_of(win.at[2], [shard[k] for k in sets[i]])
        rope = rope_of(win.at[2], [shard[k] for k in sets[i]])
        for n, k in enumerate(sets[i]):
            mask = mask_s[pl.ds(pl.multiple_of(shard[k] * 64, 64), 64), :]
            tail_s[pl.ds(T * i + 64 * n, 64), :] = key_tail(rope[64 * n:64 * n + 64], mask)

        def some(g, carry):
            columns = pl.ds(pl.multiple_of(g * 512, 512), 512)
            k_s[pl.ds(T * i, T), columns] = expand(latent, wk_s[:, columns])
            v_s[pl.ds(T * i, T), columns] = expand(latent, wv_s[:, columns])
            return carry

        lax.fori_loop(0, 4, some, 0)

    def attend(i, start, end):
        rows = pl.ds(T * i, T)

        def some(g, carry):
            tail = tail_s[rows, :]
            for h in range(8):
                head = g * 8 + h
                columns = pl.ds(pl.multiple_of(head * 128, 128), 128)
                keys = jnp.concatenate([k_s[rows, columns], tail], axis=1)
                weights = jnp.exp2(scores(qp[head], keys) + causal_s[i]).astype(BF16)
                part = jnp.dot(weights, with_ones(v_s[rows, columns]), preferred_element_type=F32)
                acc_s[head] = part if i == 0 else acc_s[head] + part
            return carry

        lax.fori_loop(start, end, some, 0)

    forward = (ctx < 14) & jnp.logical_not(before_turn)

    def earlier_shard(k):
        pl.when(ctx >= 2)(lambda: got(0, k))
        c = remote(piece(0, k), piece(0, k), send.at[40 + k], recv.at[0, k ^ 1], peers["partner"])
        c.start()
        relay_if(0, k)

    def in_time(k):
        pl.when(jnp.logical_not(turn))(lambda: earlier_shard(k))

    def late(k):
        pl.when(turn)(lambda: earlier_shard(k))

    query_at = lax.broadcasted_iota(jnp.int32, (512, 64), 0)
    ahead = query_at - lax.broadcasted_iota(jnp.int32, (512, 64), 1)
    for i in range(2):
        visible = jnp.concatenate([jnp.where(ahead >= shard[k] * 64, 0.0, -BIG) for k in sets[i]], axis=1)
        causal_s[i] = visible

    got(1, 1)
    for where in ("right", "left", "far"):
        give(1, 1, where)
    relay_if(1, 1)
    got(1, 2)
    give(1, 2, "next", forward)
    got(1, 4)
    give(1, 4, "next", forward)
    relay_if(1, 2)
    relay_if(1, 4)
    in_time(0)
    loads[3].wait()
    loads[4].wait()
    widen(0)
    late(0)
    for where in ("right", "left", "far"):
        give(0, 0, where, turn)
    attend(0, 0, 1)
    got(1, 6)
    give(1, 6, "next", forward)
    relay_if(1, 6)
    in_time(2)
    attend(0, 1, 2)
    got(1, 3)
    relay_if(1, 3)
    got(1, 5)
    relay_if(1, 5)
    in_time(4)
    got(1, 7)
    relay_if(1, 7)
    widen(1)
    late(2)
    late(4)
    earlier_shard(6)
    attend(1, 0, 1)
    for k in (1, 3):
        got(0, k)
        relay_if(0, k)
    attend(1, 1, 2)
    for k in (5, 7):
        got(0, k)
        relay_if(0, k)

    pl.when(ctx >= 1)(d1.wait_recv)
    pl.when(ctx >= 2)(d2.wait_recv)
    for k in range(8):
        place = win.at[1, shard[k]]
        remote(place, place, relay_send.at[k], relay_recv.at[k], sibling).wait_recv()
    for c, condition in started:
        if condition is None:
            c.wait_send()
        else:
            pl.when(condition)(c.wait_send)
    for k in (0, 2, 4, 6):
        remote(piece(0, k), piece(0, k), send.at[40 + k], recv.at[0, k ^ 1], peers["partner"]).wait_send()
    for k in range(8):
        relay(k).wait_send()
    pl.when(ctx < 14)(d2.wait_send)
    pl.when(ctx < 15)(d1.wait_send)


def gather(latent, docs, queries, w_key, w_value):
    vmem, hbm = pl.BlockSpec(memory_space=pltpu.VMEM), pl.BlockSpec(memory_space=pltpu.HBM)
    operands = [pltpu.with_memory_space_constraint(a, pltpu.HBM) for a in (latent, docs, queries, w_key, w_value)]
    return pl.pallas_call(
        gather_kernel,
        out_shape=(
            pltpu.VMEM((3, 8, 32, 1152), BF16),
            pltpu.VMEM((3, 4, 128), jnp.int32),
            pltpu.VMEM((HEADS, 512, 256), BF16),
            pltpu.VMEM((512, 2048), BF16),
            pltpu.VMEM((512, 2048), BF16),
            pltpu.VMEM((HEADS, 512, 256), F32),
        ),
        in_specs=[hbm] * 5,
        out_specs=(vmem,) * 6,
        scratch_shapes=[
            pltpu.VMEM((64, 576), BF16),
            pltpu.VMEM((32, 1152), BF16),
            pltpu.VMEM((512, 3072), BF16),
            pltpu.VMEM((512, HEADS * 128), BF16),
            pltpu.VMEM((512, HEADS * 128), BF16),
            pltpu.VMEM((512, 128), BF16),
            pltpu.VMEM((512, 128), BF16),
            pltpu.VMEM((512, 128), BF16),
            pltpu.VMEM((2, 512, T), F32),
            pltpu.SemaphoreType.DMA((48,)),
            pltpu.SemaphoreType.DMA((2, 8)),
            pltpu.SemaphoreType.DMA((8,)),
            pltpu.SemaphoreType.DMA((8,)),
            pltpu.SemaphoreType.DMA((2,)),
            pltpu.SemaphoreType.DMA((2,)),
            pltpu.SemaphoreType.DMA((5,)),
        ],
        compiler_params=pltpu.CompilerParams(collective_id=0, has_side_effects=True, vmem_limit_bytes=20 * 2**20),
    )(*operands)


def earlier_kernel(win_ref, docs_ref, qp, wk_ref, wv_ref, acc_ref, out_ref, o_s, k_s, v_s, k2_s, v2_s, tail_s, rng_s, out_sem):
    wide = ((k_s, v_s), (k2_s, v2_s))

    def document(row):
        b, rest = divmod(row, 512)
        return docs_ref[b, rest // 128, rest % 128]

    def first_chunk(block):
        lowest = jnp.int32(4)
        for c in reversed(range(block, 4)):
            lowest = jnp.where(document(c * T + T - 1) == document(1024 + block * T), c, lowest)
        return lowest

    first, both = first_chunk(0), first_chunk(1) < 4
    window = win_ref.reshape(24, 32, 1152)

    def tails(start, end):
        for r in range(start, end):
            rope = rope_of(window, (2 * r, 2 * r + 1))
            tail_s[pl.ds(128 * r, 128), :] = key_tail(rope, document_mask(docs_ref[r // 4, r % 4:r % 4 + 1, :]))

    rng_s[0] = jnp.ones((T, 128), F32)
    rng_s[1] = jnp.ones((T, 128), F32)

    def store(head, row, acc):
        total = acc[:, 128:]
        o_s[head, pl.ds(row, acc.shape[0]), :] = (acc[:, :128] / total).astype(BF16)
        for t in range(acc.shape[0] // T):
            rng_s[0] = jnp.minimum(rng_s[0], total[t * T:(t + 1) * T])
            rng_s[1] = jnp.maximum(rng_s[1], total[t * T:(t + 1) * T])

    def write(head):
        return pltpu.make_async_copy(o_s.at[head], out_ref.at[:, pl.ds(pl.multiple_of(head * 128, 128), 128)], out_sem.at[head])

    def run(start, reach):
        count = 4 - start
        every = pl.ds(0, count * T)

        def widen(head, heads, k, v):
            part = pl.ds(pl.multiple_of(head * 128, 128), heads * 128)
            latent = rows_of(window, range(4 * start, 16))
            k[every, pl.ds(0, heads * 128)] = expand(latent, wk_ref[:, part])
            v[every, pl.ds(0, heads * 128)] = expand(latent, wv_ref[:, part])

        def attend(first_head, heads, k, v):
            for h in range(heads):
                head = first_head + h
                own = slice(h * 128, h * 128 + 128)
                acc = acc_ref[head, pl.ds(0, reach), :]
                for c in range(count):
                    rows = pl.ds(c * T, T)
                    keys = jnp.concatenate([k[rows, own], tail_s[pl.ds((start + c) * T, T), :]], axis=1)
                    weights = jnp.exp2(scores(qp[head, pl.ds(0, reach), :], keys)).astype(BF16)
                    acc = acc + jnp.dot(weights, with_ones(v[rows, own]), preferred_element_type=F32)
                store(head, 0, acc)
                if reach < 512:
                    store(head, reach, acc_ref[head, pl.ds(reach, 512 - reach), :])
                write(head).start()

        if count:
            tails(2 * start, 8)

        if (start, reach) in UNROLLED:
            slots = ((k_s, v_s), (k2_s, v2_s))
            widen(0, SOME, *slots[0])
            for i in range(HEADS // SOME):
                if (i + 1) * SOME < HEADS:
                    widen((i + 1) * SOME, SOME, *slots[(i + 1) % 2])
                attend(i * SOME, SOME, *slots[i % 2])
        else:
            def step(i, carry):
                if count:
                    widen(4 * i, 4, k_s, v_s)
                attend(4 * i, 4, k_s, v_s)
                return carry

            lax.fori_loop(0, HEADS // 4, step, 0)

    for start in range(5):
        for reach in ((512,) if start == 4 else (256,) if start == 0 else (256, 512)):
            chosen = first == start
            if start < 4:
                chosen = chosen & (both if reach == 512 else jnp.logical_not(both))
            pl.when(chosen)(functools.partial(run, start, reach))
    for head in range(HEADS):
        write(head).wait()

    inside = (jnp.min(rng_s[0]) >= LOW) & (jnp.max(rng_s[1]) <= HIGH)

    @pl.when(jnp.logical_not(inside))
    def _():
        tails(0, 12)

        def one(head, carry):
            part = pl.ds(pl.multiple_of(head * 128, 128), 128)
            own = pl.ds(0, 128)

            def widen(c, carry):
                latent = rows_of(window, [4 * c + i for i in range(4)])
                rows = pl.ds(pl.multiple_of(c * T, T), T)
                k_s[rows, own] = expand(latent, wk_ref[:, part])
                v_s[rows, own] = expand(latent, wv_ref[:, part])
                return carry

            lax.fori_loop(first, 6, widen, 0)
            causal = causal_mask()
            for qb in range(2):
                end = 4 + qb

                def body(c, state):
                    peak, acc = state
                    rows = pl.ds(pl.multiple_of(c * T, T), T)
                    keys = jnp.concatenate([k_s[rows, own], tail_s[rows, :]], axis=1)
                    s = scores(qp[head, pl.ds(qb * T, T), :], keys)
                    s = jnp.where(causal | (c < end), s, -BIG)
                    new = jnp.maximum(peak, jnp.max(s, axis=1, keepdims=True))
                    weights = jnp.exp2(s - new).astype(BF16)
                    t = jnp.dot(weights, with_ones(v_s[rows, own]), preferred_element_type=F32)
                    return new, acc * jnp.exp2(peak - new) + t

                initial = (jnp.full((T, 1), -BIG, F32), jnp.zeros((T, 256), F32))
                _, acc = lax.fori_loop(first, end + 1, body, initial)
                o_s[head, pl.ds(qb * T, T), :] = (acc[:, :128] / acc[:, 128:]).astype(BF16)
            write(head).start()
            write(head).wait()
            return carry

        lax.fori_loop(0, HEADS, one, 0)


def earlier(window, docs, qp, w_key, w_value, acc):
    vmem, hbm = pl.BlockSpec(memory_space=pltpu.VMEM), pl.BlockSpec(memory_space=pltpu.HBM)
    return pl.pallas_call(
        earlier_kernel,
        out_shape=jax.ShapeDtypeStruct((512, 2048), BF16),
        in_specs=[vmem] * 6,
        out_specs=hbm,
        scratch_shapes=[
            pltpu.VMEM((HEADS, 512, 128), BF16),
            pltpu.VMEM((1536, 512), BF16),
            pltpu.VMEM((1536, 512), BF16),
            pltpu.VMEM((1024, 512), BF16),
            pltpu.VMEM((1024, 512), BF16),
            pltpu.VMEM((1536, 128), BF16),
            pltpu.VMEM((2, T, 128), F32),
            pltpu.SemaphoreType.DMA((HEADS,)),
        ],
        compiler_params=pltpu.CompilerParams(vmem_limit_bytes=26 * 2**20),
    )(window, docs, qp, w_key, w_value, acc)


def on_device(queries, latent_cache, doc_ids, w_key, w_value):
    window, docs, qp, wk, wv, acc = gather(latent_cache, doc_ids.reshape(4, 128), queries, w_key, w_value)
    return earlier(window, docs, qp, wk, wv, acc)


def solution(mesh):
    placed = (P("ctx", "dp"), P(("ctx", "dp"), None), P("ctx"), P(None, "dp"), P(None, "dp"))
    return jax.shard_map(on_device, mesh=mesh, in_specs=placed, out_specs=P("ctx", "dp"), check_vma=False)
```

```python
import functools
import math

import jax
import jax.numpy as jnp
from jax import lax
from jax.experimental import pallas as pl
from jax.experimental.pallas import tpu as pltpu
from jax.sharding import PartitionSpec as P

MESH = pl.DeviceIdType.MESH
BF16, F32 = jnp.bfloat16, jnp.float32
HEADS = 16
UNROLLED = ((1, 512), (0, 256))
SOME = 2
T = 256
BIG = 1e30
SCALE = math.log2(math.e) / math.sqrt(192)
LOW, HIGH = 2.0 ** -60, 2.0 ** 100
NT = (((1,), (1,)), ((), ()))


def scores(query, keys):
    return lax.dot_general(query, keys, NT, preferred_element_type=F32) * SCALE


def with_ones(value):
    return jnp.concatenate([value, jnp.ones((value.shape[0], 128), BF16)], axis=1)


def expand(rows, weight):
    return jnp.dot(rows, weight, preferred_element_type=F32).astype(BF16)


def documents_down(row):
    return jnp.transpose(jnp.broadcast_to(row, (128, 128)).astype(F32)).astype(jnp.int32)


def document_mask(row):
    lane = lax.broadcasted_iota(jnp.int32, (128, 128), 1)
    other = (lane >= 64) & (lane < 80) & (documents_down(row) != lane - 64)
    return jnp.where(other, -BIG, 0.0).astype(BF16)


def key_tail(rope, mask):
    return jnp.concatenate([rope, mask[:, 64:]], axis=1)


def query_tail(row):
    lane = lax.broadcasted_iota(jnp.int32, (128, 128), 1)
    return (documents_down(row) == lane - 64).astype(F32).astype(BF16)


def causal_mask():
    return lax.broadcasted_iota(jnp.int32, (T, T), 1) <= lax.broadcasted_iota(jnp.int32, (T, T), 0)


def rows_of(window, shards):
    return jnp.concatenate([window[k, :, 512 * j:512 * j + 512] for k in shards for j in range(2)], axis=0)


def rope_of(window, shards):
    packed = [window[k, :, 1024:] for k in shards]
    return jnp.concatenate([p[:, 64 * j:64 * j + 64] for p in packed for j in range(2)], axis=0)


def gather_kernel(lat_ref, docs_ref, q_ref, wk_ref, wv_ref,
                  win, docs_s, qp, wk_s, wv_s, acc_s,
                  lat_s, own_s, q_s, k_s, v_s, tail_s, qtail_s, mask_s, causal_s,
                  send, recv, relay_send, relay_recv, misc_send, misc_recv, load_sem):
    ctx, dp = lax.axis_index("ctx"), lax.axis_index("dp")
    x, y, core = dp // 2, dp % 2, ctx % 2
    right_x, left_x, far_x = (x + 1) % 4, (x + 3) % 4, (x + 2) % 4
    next1, next2 = ((ctx + 1) % 16, dp), ((ctx + 2) % 16, dp)
    prev1, prev2 = ((ctx + 15) % 16, dp), ((ctx + 14) % 16, dp)
    sibling = (ctx + 1 - 2 * core, dp)
    peers = {
        "partner": (ctx, x * 2 + 1 - y), "right": (ctx, right_x * 2 + y), "left": (ctx, left_x * 2 + y),
        "far": (ctx, far_x * 2 + y), "next": next2}
    turn = ctx // 2 == 4
    before_turn = ctx // 2 == 3
    shard = [column * 2 + row for column in (x, left_x, right_x, far_x) for row in (y, 1 - y)]
    kind_there = {
        "partner": lambda k: k ^ 1, "right": lambda k: 2 + k, "left": lambda k: 4 + k, "far": lambda k: 6 + k,
        "next": lambda k: k}

    barrier = pltpu.get_barrier_semaphore()

    def greet(peer):
        pl.semaphore_signal(barrier, inc=1, device_id=peer, device_id_type=MESH)

    for name in ("partner", "right", "left", "far"):
        greet(peers[name])
    pl.when(ctx >= 1)(lambda: greet(prev1))
    pl.when(ctx >= 2)(lambda: greet(prev2))
    pl.when(core == 0)(lambda: greet(sibling))

    loads = [pltpu.make_async_copy(src, dst, load_sem.at[i]) for i, (src, dst) in enumerate((
        (lat_ref, lat_s), (docs_ref, docs_s.at[2]), (q_ref, q_s), (wk_ref, wk_s), (wv_ref, wv_s)))]
    for c in loads:
        c.start()

    def remote(src, dst, send_sem, recv_sem, peer):
        return pltpu.make_async_remote_copy(
            src_ref=src, dst_ref=dst, send_sem=send_sem, recv_sem=recv_sem, device_id=peer, device_id_type=MESH)

    def piece(w, k):
        return win.at[2 * w, shard[k]]

    started = []

    def give(w, k, where, condition=None):
        to = 0 if where == "next" else w
        src = own_s if (w, k) == (1, 0) else piece(w, k)
        c = remote(src, win.at[2 * to, shard[k]], send.at[len(started)], recv.at[to, kind_there[where](k)], peers[where])
        started.append((c, condition))
        if condition is None:
            c.start()
        else:
            pl.when(condition)(c.start)

    def got(w, k):
        remote(piece(w, k), piece(w, k), send.at[0], recv.at[w, k], sibling).wait_recv()

    def relay(k):
        return remote(win.at[2 - 2 * core, shard[k]], win.at[1, shard[k]], relay_send.at[k], relay_recv.at[k], sibling)

    def relay_if(w, k):
        pl.when(core == 1 - w)(lambda: relay(k).start())

    loads[0].wait()
    packed = jnp.concatenate(
        [lat_s[:32, :512], lat_s[32:, :512], lat_s[:32, 512:], lat_s[32:, 512:]], axis=1)
    own_s[...] = packed
    win[2, dp] = packed

    loads[1].wait()
    for r in range(4):
        qtail_s[pl.ds(128 * r, 128), :] = query_tail(docs_s[2, r:r + 1, :])
        mask_s[pl.ds(128 * r, 128), :] = document_mask(docs_s[2, r:r + 1, :])

    @pl.when(ctx < 2)
    def _():
        docs_s[0] = jnp.full((4, 128), -1, jnp.int32)
        for k in (0, 2, 4, 6):
            win[0, shard[k]] = packed

    @pl.when(ctx < 1)
    def _():
        docs_s[1] = jnp.full((4, 128), -1, jnp.int32)

    d1 = remote(docs_ref, docs_s.at[1], misc_send.at[0], misc_recv.at[0], next1)
    d2 = remote(docs_ref, docs_s.at[0], misc_send.at[1], misc_recv.at[1], next2)

    forward = (ctx < 14) & jnp.logical_not(before_turn)
    pl.semaphore_wait(barrier, 4 + jnp.where(ctx < 15, 1, 0) + jnp.where(ctx < 14, 1, 0) + core)

    give(1, 0, "next", before_turn)
    for where in ("partner", "right", "left", "far"):
        give(1, 0, where)
    give(1, 0, "next", forward)
    pl.when(ctx < 14)(d2.start)
    pl.when(ctx < 15)(d1.start)
    relay_if(1, 0)

    loads[2].wait()
    qtail = qtail_s[...]

    def prepare(p, carry):
        a, b, c = [q_s[:, pl.ds(pl.multiple_of(p * 384 + 128 * i, 128), 128)] for i in range(3)]
        qp[2 * p, :, :128] = a
        qp[2 * p, :, 128:] = jnp.concatenate([b[:, :64], qtail[:, 64:]], axis=1)
        qp[2 * p + 1, :, :128] = jnp.concatenate([b[:, 64:], c[:, :64]], axis=1)
        qp[2 * p + 1, :, 128:] = jnp.concatenate([c[:, 64:], qtail[:, 64:]], axis=1)
        return carry

    lax.fori_loop(0, HEADS // 2, prepare, 0)

    sets = ((0, 1, 2, 4), (3, 5, 6, 7))

    def widen(i):
        latent = rows_of(win.at[2], [shard[k] for k in sets[i]])
        rope = rope_of(win.at[2], [shard[k] for k in sets[i]])
        for n, k in enumerate(sets[i]):
            mask = mask_s[pl.ds(pl.multiple_of(shard[k] * 64, 64), 64), :]
            tail_s[pl.ds(T * i + 64 * n, 64), :] = key_tail(rope[64 * n:64 * n + 64], mask)

        def some(g, carry):
            columns = pl.ds(pl.multiple_of(g * 512, 512), 512)
            k_s[pl.ds(T * i, T), columns] = expand(latent, wk_s[:, columns])
            v_s[pl.ds(T * i, T), columns] = expand(latent, wv_s[:, columns])
            return carry

        lax.fori_loop(0, 4, some, 0)

    def attend(i, start, end):
        rows = pl.ds(T * i, T)

        def some(g, carry):
            tail = tail_s[rows, :]
            for h in range(8):
                head = g * 8 + h
                columns = pl.ds(pl.multiple_of(head * 128, 128), 128)
                keys = jnp.concatenate([k_s[rows, columns], tail], axis=1)
                weights = jnp.exp2(scores(qp[head], keys) + causal_s[i]).astype(BF16)
                part = jnp.dot(weights, with_ones(v_s[rows, columns]), preferred_element_type=F32)
                acc_s[head] = part if i == 0 else acc_s[head] + part
            return carry

        lax.fori_loop(start, end, some, 0)

    def to_partner(k):
        return remote(piece(0, k), piece(0, k), send.at[40 + k], recv.at[0, k ^ 1], peers["partner"])

    def earlier_shard(k, pass_on=True):
        pl.when(ctx >= 2)(lambda: got(0, k))
        if pass_on:
            to_partner(k).start()
        relay_if(0, k)

    straight = jnp.logical_not(turn)

    def in_time(k):
        pl.when(straight)(lambda: earlier_shard(k))

    def late(k, pass_on):
        pl.when(turn)(lambda: earlier_shard(k, pass_on))

    def partner_shard():
        got(0, 1)
        relay_if(0, 1)

    query_at = lax.broadcasted_iota(jnp.int32, (512, 64), 0)
    ahead = query_at - lax.broadcasted_iota(jnp.int32, (512, 64), 1)
    for i in range(2):
        visible = jnp.concatenate([jnp.where(ahead >= shard[k] * 64, 0.0, -BIG) for k in sets[i]], axis=1)
        causal_s[i] = visible

    got(1, 1)
    for where in ("right", "left", "far"):
        give(1, 1, where)
    relay_if(1, 1)
    got(1, 2)
    give(1, 2, "next", forward)
    got(1, 4)
    give(1, 4, "next", forward)
    relay_if(1, 2)
    relay_if(1, 4)
    in_time(0)
    loads[3].wait()
    loads[4].wait()
    widen(0)
    late(0, True)
    for where in ("far", "right", "left"):
        give(0, 0, where, turn)
    attend(0, 0, 1)
    got(1, 6)
    give(1, 6, "next", forward)
    relay_if(1, 6)
    in_time(2)
    attend(0, 1, 2)
    got(1, 3)
    relay_if(1, 3)
    got(1, 5)
    relay_if(1, 5)
    in_time(4)
    got(1, 7)
    relay_if(1, 7)
    pl.when(turn)(partner_shard)
    for where in ("right", "left"):
        give(0, 1, where, turn)
    widen(1)
    late(2, False)
    late(4, False)
    earlier_shard(6)
    attend(1, 0, 1)
    pl.when(straight)(partner_shard)
    got(0, 3)
    relay_if(0, 3)
    attend(1, 1, 2)
    for k in (5, 7):
        got(0, k)
        relay_if(0, k)

    pl.when(ctx >= 1)(d1.wait_recv)
    pl.when(ctx >= 2)(d2.wait_recv)
    for k in range(8):
        place = win.at[1, shard[k]]
        remote(place, place, relay_send.at[k], relay_recv.at[k], sibling).wait_recv()
    for c, condition in started:
        if condition is None:
            c.wait_send()
        else:
            pl.when(condition)(c.wait_send)
    for k in (0, 6):
        to_partner(k).wait_send()
    for k in (2, 4):
        pl.when(straight)(to_partner(k).wait_send)
    for k in range(8):
        relay(k).wait_send()
    pl.when(ctx < 14)(d2.wait_send)
    pl.when(ctx < 15)(d1.wait_send)


def gather(latent, docs, queries, w_key, w_value):
    vmem, hbm = pl.BlockSpec(memory_space=pltpu.VMEM), pl.BlockSpec(memory_space=pltpu.HBM)
    operands = [pltpu.with_memory_space_constraint(a, pltpu.HBM) for a in (latent, docs, queries, w_key, w_value)]
    return pl.pallas_call(
        gather_kernel,
        out_shape=(
            pltpu.VMEM((3, 8, 32, 1152), BF16),
            pltpu.VMEM((3, 4, 128), jnp.int32),
            pltpu.VMEM((HEADS, 512, 256), BF16),
            pltpu.VMEM((512, 2048), BF16),
            pltpu.VMEM((512, 2048), BF16),
            pltpu.VMEM((HEADS, 512, 256), F32),
        ),
        in_specs=[hbm] * 5,
        out_specs=(vmem,) * 6,
        scratch_shapes=[
            pltpu.VMEM((64, 576), BF16),
            pltpu.VMEM((32, 1152), BF16),
            pltpu.VMEM((512, 3072), BF16),
            pltpu.VMEM((512, HEADS * 128), BF16),
            pltpu.VMEM((512, HEADS * 128), BF16),
            pltpu.VMEM((512, 128), BF16),
            pltpu.VMEM((512, 128), BF16),
            pltpu.VMEM((512, 128), BF16),
            pltpu.VMEM((2, 512, T), F32),
            pltpu.SemaphoreType.DMA((48,)),
            pltpu.SemaphoreType.DMA((2, 8)),
            pltpu.SemaphoreType.DMA((8,)),
            pltpu.SemaphoreType.DMA((8,)),
            pltpu.SemaphoreType.DMA((2,)),
            pltpu.SemaphoreType.DMA((2,)),
            pltpu.SemaphoreType.DMA((5,)),
        ],
        compiler_params=pltpu.CompilerParams(collective_id=0, has_side_effects=True, vmem_limit_bytes=20 * 2**20),
    )(*operands)


def earlier_kernel(win_ref, docs_ref, qp, wk_ref, wv_ref, acc_ref, out_ref, o_s, k_s, v_s, k2_s, v2_s, tail_s, rng_s, out_sem):
    wide = ((k_s, v_s), (k2_s, v2_s))

    def document(row):
        b, rest = divmod(row, 512)
        return docs_ref[b, rest // 128, rest % 128]

    def first_chunk(block):
        lowest = jnp.int32(4)
        for c in reversed(range(block, 4)):
            lowest = jnp.where(document(c * T + T - 1) == document(1024 + block * T), c, lowest)
        return lowest

    first, both = first_chunk(0), first_chunk(1) < 4
    window = win_ref.reshape(24, 32, 1152)

    def tails(start, end):
        for r in range(start, end):
            rope = rope_of(window, (2 * r, 2 * r + 1))
            tail_s[pl.ds(128 * r, 128), :] = key_tail(rope, document_mask(docs_ref[r // 4, r % 4:r % 4 + 1, :]))

    rng_s[0] = jnp.ones((T, 128), F32)
    rng_s[1] = jnp.ones((T, 128), F32)

    def store(head, row, acc):
        total = acc[:, 128:]
        o_s[head, pl.ds(row, acc.shape[0]), :] = (acc[:, :128] / total).astype(BF16)
        for t in range(acc.shape[0] // T):
            rng_s[0] = jnp.minimum(rng_s[0], total[t * T:(t + 1) * T])
            rng_s[1] = jnp.maximum(rng_s[1], total[t * T:(t + 1) * T])

    def write(head):
        return pltpu.make_async_copy(o_s.at[head], out_ref.at[:, pl.ds(pl.multiple_of(head * 128, 128), 128)], out_sem.at[head])

    def run(start, reach):
        count = 4 - start
        every = pl.ds(0, count * T)

        def widen(head, heads, k, v):
            part = pl.ds(pl.multiple_of(head * 128, 128), heads * 128)
            latent = rows_of(window, range(4 * start, 16))
            k[every, pl.ds(0, heads * 128)] = expand(latent, wk_ref[:, part])
            v[every, pl.ds(0, heads * 128)] = expand(latent, wv_ref[:, part])

        def attend(first_head, heads, k, v):
            for h in range(heads):
                head = first_head + h
                own = slice(h * 128, h * 128 + 128)
                acc = acc_ref[head, pl.ds(0, reach), :]
                for c in range(count):
                    rows = pl.ds(c * T, T)
                    keys = jnp.concatenate([k[rows, own], tail_s[pl.ds((start + c) * T, T), :]], axis=1)
                    weights = jnp.exp2(scores(qp[head, pl.ds(0, reach), :], keys)).astype(BF16)
                    acc = acc + jnp.dot(weights, with_ones(v[rows, own]), preferred_element_type=F32)
                store(head, 0, acc)
                if reach < 512:
                    store(head, reach, acc_ref[head, pl.ds(reach, 512 - reach), :])
                write(head).start()

        if count:
            tails(2 * start, 8)

        if (start, reach) in UNROLLED:
            slots = ((k_s, v_s), (k2_s, v2_s))
            widen(0, SOME, *slots[0])
            for i in range(HEADS // SOME):
                if (i + 1) * SOME < HEADS:
                    widen((i + 1) * SOME, SOME, *slots[(i + 1) % 2])
                attend(i * SOME, SOME, *slots[i % 2])
        else:
            def step(i, carry):
                if count:
                    widen(4 * i, 4, k_s, v_s)
                attend(4 * i, 4, k_s, v_s)
                return carry

            lax.fori_loop(0, HEADS // 4, step, 0)

    for start in range(5):
        for reach in ((512,) if start == 4 else (256,) if start == 0 else (256, 512)):
            chosen = first == start
            if start < 4:
                chosen = chosen & (both if reach == 512 else jnp.logical_not(both))
            pl.when(chosen)(functools.partial(run, start, reach))
    for head in range(HEADS):
        write(head).wait()

    inside = (jnp.min(rng_s[0]) >= LOW) & (jnp.max(rng_s[1]) <= HIGH)

    @pl.when(jnp.logical_not(inside))
    def _():
        tails(0, 12)

        def one(head, carry):
            part = pl.ds(pl.multiple_of(head * 128, 128), 128)
            own = pl.ds(0, 128)

            def widen(c, carry):
                latent = rows_of(window, [4 * c + i for i in range(4)])
                rows = pl.ds(pl.multiple_of(c * T, T), T)
                k_s[rows, own] = expand(latent, wk_ref[:, part])
                v_s[rows, own] = expand(latent, wv_ref[:, part])
                return carry

            lax.fori_loop(first, 6, widen, 0)
            causal = causal_mask()
            for qb in range(2):
                end = 4 + qb

                def body(c, state):
                    peak, acc = state
                    rows = pl.ds(pl.multiple_of(c * T, T), T)
                    keys = jnp.concatenate([k_s[rows, own], tail_s[rows, :]], axis=1)
                    s = scores(qp[head, pl.ds(qb * T, T), :], keys)
                    s = jnp.where(causal | (c < end), s, -BIG)
                    new = jnp.maximum(peak, jnp.max(s, axis=1, keepdims=True))
                    weights = jnp.exp2(s - new).astype(BF16)
                    t = jnp.dot(weights, with_ones(v_s[rows, own]), preferred_element_type=F32)
                    return new, acc * jnp.exp2(peak - new) + t

                initial = (jnp.full((T, 1), -BIG, F32), jnp.zeros((T, 256), F32))
                _, acc = lax.fori_loop(first, end + 1, body, initial)
                o_s[head, pl.ds(qb * T, T), :] = (acc[:, :128] / acc[:, 128:]).astype(BF16)
            write(head).start()
            write(head).wait()
            return carry

        lax.fori_loop(0, HEADS, one, 0)


def earlier(window, docs, qp, w_key, w_value, acc):
    vmem, hbm = pl.BlockSpec(memory_space=pltpu.VMEM), pl.BlockSpec(memory_space=pltpu.HBM)
    return pl.pallas_call(
        earlier_kernel,
        out_shape=jax.ShapeDtypeStruct((512, 2048), BF16),
        in_specs=[vmem] * 6,
        out_specs=hbm,
        scratch_shapes=[
            pltpu.VMEM((HEADS, 512, 128), BF16),
            pltpu.VMEM((1536, 512), BF16),
            pltpu.VMEM((1536, 512), BF16),
            pltpu.VMEM((1024, 512), BF16),
            pltpu.VMEM((1024, 512), BF16),
            pltpu.VMEM((1536, 128), BF16),
            pltpu.VMEM((2, T, 128), F32),
            pltpu.SemaphoreType.DMA((HEADS,)),
        ],
        compiler_params=pltpu.CompilerParams(vmem_limit_bytes=26 * 2**20),
    )(window, docs, qp, w_key, w_value, acc)


def on_device(queries, latent_cache, doc_ids, w_key, w_value):
    window, docs, qp, wk, wv, acc = gather(latent_cache, doc_ids.reshape(4, 128), queries, w_key, w_value)
    return earlier(window, docs, qp, wk, wv, acc)


def solution(mesh):
    placed = (P("ctx", "dp"), P(("ctx", "dp"), None), P("ctx"), P(None, "dp"), P(None, "dp"))
    return jax.shard_map(on_device, mesh=mesh, in_specs=placed, out_specs=P("ctx", "dp"), check_vma=False)
```

```python
import functools
import math

import jax
import jax.numpy as jnp
from jax import lax
from jax.experimental import pallas as pl
from jax.experimental.pallas import tpu as pltpu
from jax.sharding import PartitionSpec as P

MESH = pl.DeviceIdType.MESH
BF16, F32 = jnp.bfloat16, jnp.float32
HEADS = 16
UNROLLED = ((1, 512), (0, 256))
SOME = 2
T = 256
BIG = 1e30
SCALE = math.log2(math.e) / math.sqrt(192)
LOW, HIGH = 2.0 ** -60, 2.0 ** 100
NT = (((1,), (1,)), ((), ()))


def scores(query, keys):
    return lax.dot_general(query, keys, NT, preferred_element_type=F32) * SCALE


def with_ones(value):
    return jnp.concatenate([value, jnp.ones((value.shape[0], 128), BF16)], axis=1)


def expand(rows, weight):
    return jnp.dot(rows, weight, preferred_element_type=F32).astype(BF16)


def documents_down(row):
    return jnp.transpose(jnp.broadcast_to(row, (128, 128)).astype(F32)).astype(jnp.int32)


def document_mask(row):
    lane = lax.broadcasted_iota(jnp.int32, (128, 128), 1)
    other = (lane >= 64) & (lane < 80) & (documents_down(row) != lane - 64)
    return jnp.where(other, -BIG, 0.0).astype(BF16)


def key_tail(rope, mask):
    return jnp.concatenate([rope, mask[:, 64:]], axis=1)


def query_tail(row):
    lane = lax.broadcasted_iota(jnp.int32, (128, 128), 1)
    return (documents_down(row) == lane - 64).astype(F32).astype(BF16)


def causal_mask():
    return lax.broadcasted_iota(jnp.int32, (T, T), 1) <= lax.broadcasted_iota(jnp.int32, (T, T), 0)


def rows_of(window, shards):
    return jnp.concatenate([window[k, :, 512 * j:512 * j + 512] for k in shards for j in range(2)], axis=0)


def rope_of(window, shards):
    packed = [window[k, :, 1024:] for k in shards]
    return jnp.concatenate([p[:, 64 * j:64 * j + 64] for p in packed for j in range(2)], axis=0)


def gather_kernel(lat_ref, docs_ref, q_ref, wk_ref, wv_ref,
                  win, docs_s, qp, wk_s, wv_s, acc_s,
                  lat_s, own_s, q_s, k_s, v_s, tail_s, qtail_s, mask_s, causal_s,
                  send, recv, relay_send, relay_recv, misc_send, misc_recv, load_sem):
    ctx, dp = lax.axis_index("ctx"), lax.axis_index("dp")
    x, y, core = dp // 2, dp % 2, ctx % 2
    right_x, left_x, far_x = (x + 1) % 4, (x + 3) % 4, (x + 2) % 4
    next1, next2 = ((ctx + 1) % 16, dp), ((ctx + 2) % 16, dp)
    prev1, prev2 = ((ctx + 15) % 16, dp), ((ctx + 14) % 16, dp)
    sibling = (ctx + 1 - 2 * core, dp)
    peers = {
        "partner": (ctx, x * 2 + 1 - y), "right": (ctx, right_x * 2 + y), "left": (ctx, left_x * 2 + y),
        "far": (ctx, far_x * 2 + y), "next": next2}
    turn = ctx // 2 == 4
    before_turn = ctx // 2 == 3
    shard = [column * 2 + row for column in (x, left_x, right_x, far_x) for row in (y, 1 - y)]
    kind_there = {
        "partner": lambda k: k ^ 1, "right": lambda k: 2 + k, "left": lambda k: 4 + k, "far": lambda k: 6 + k,
        "next": lambda k: k}

    barrier = pltpu.get_barrier_semaphore()

    def greet(peer):
        pl.semaphore_signal(barrier, inc=1, device_id=peer, device_id_type=MESH)

    for name in ("partner", "right", "left", "far"):
        greet(peers[name])
    pl.when(ctx >= 1)(lambda: greet(prev1))
    pl.when(ctx >= 2)(lambda: greet(prev2))
    pl.when(core == 0)(lambda: greet(sibling))

    loads = [pltpu.make_async_copy(src, dst, load_sem.at[i]) for i, (src, dst) in enumerate((
        (lat_ref, lat_s), (docs_ref, docs_s.at[2]), (q_ref, q_s), (wk_ref, wk_s), (wv_ref, wv_s)))]
    for c in loads:
        c.start()

    def remote(src, dst, send_sem, recv_sem, peer):
        return pltpu.make_async_remote_copy(
            src_ref=src, dst_ref=dst, send_sem=send_sem, recv_sem=recv_sem, device_id=peer, device_id_type=MESH)

    def piece(w, k):
        return win.at[2 * w, shard[k]]

    started = []

    def give(w, k, where, condition=None):
        to = 0 if where == "next" else w
        src = own_s if (w, k) == (1, 0) else piece(w, k)
        c = remote(src, win.at[2 * to, shard[k]], send.at[len(started)], recv.at[to, kind_there[where](k)], peers[where])
        started.append((c, condition))
        if condition is None:
            c.start()
        else:
            pl.when(condition)(c.start)

    def got(w, k):
        remote(piece(w, k), piece(w, k), send.at[0], recv.at[w, k], sibling).wait_recv()

    def relay(k):
        return remote(win.at[2 - 2 * core, shard[k]], win.at[1, shard[k]], relay_send.at[k], relay_recv.at[k], sibling)

    def relay_if(w, k):
        pl.when(core == 1 - w)(lambda: relay(k).start())

    loads[0].wait()
    packed = jnp.concatenate(
        [lat_s[:32, :512], lat_s[32:, :512], lat_s[:32, 512:], lat_s[32:, 512:]], axis=1)
    own_s[...] = packed
    win[2, dp] = packed

    d1 = remote(docs_ref, docs_s.at[1], misc_send.at[0], misc_recv.at[0], next1)
    d2 = remote(docs_ref, docs_s.at[0], misc_send.at[1], misc_recv.at[1], next2)

    forward = (ctx < 14) & jnp.logical_not(before_turn)
    pl.semaphore_wait(barrier, 4 + jnp.where(ctx < 15, 1, 0) + jnp.where(ctx < 14, 1, 0) + core)

    give(1, 0, "next", before_turn)
    for where in ("partner", "right", "left", "far"):
        give(1, 0, where)
    give(1, 0, "next", forward)
    pl.when(ctx < 14)(d2.start)
    pl.when(ctx < 15)(d1.start)
    relay_if(1, 0)

    loads[1].wait()
    for r in range(4):
        qtail_s[pl.ds(128 * r, 128), :] = query_tail(docs_s[2, r:r + 1, :])
        mask_s[pl.ds(128 * r, 128), :] = document_mask(docs_s[2, r:r + 1, :])

    @pl.when(ctx < 2)
    def _():
        docs_s[0] = jnp.full((4, 128), -1, jnp.int32)
        for k in (0, 2, 4, 6):
            win[0, shard[k]] = own_s[...]

    @pl.when(ctx < 1)
    def _():
        docs_s[1] = jnp.full((4, 128), -1, jnp.int32)

    loads[2].wait()
    qtail = qtail_s[...]

    def prepare(p, carry):
        a, b, c = [q_s[:, pl.ds(pl.multiple_of(p * 384 + 128 * i, 128), 128)] for i in range(3)]
        qp[2 * p, :, :128] = a
        qp[2 * p, :, 128:] = jnp.concatenate([b[:, :64], qtail[:, 64:]], axis=1)
        qp[2 * p + 1, :, :128] = jnp.concatenate([b[:, 64:], c[:, :64]], axis=1)
        qp[2 * p + 1, :, 128:] = jnp.concatenate([c[:, 64:], qtail[:, 64:]], axis=1)
        return carry

    lax.fori_loop(0, HEADS // 2, prepare, 0)

    sets = ((0, 1, 2, 4), (3, 5, 6, 7))

    def tails(i):
        rope = rope_of(win.at[2], [shard[k] for k in sets[i]])
        for n, k in enumerate(sets[i]):
            mask = mask_s[pl.ds(pl.multiple_of(shard[k] * 64, 64), 64), :]
            tail_s[pl.ds(T * i + 64 * n, 64), :] = key_tail(rope[64 * n:64 * n + 64], mask)

    def widen(i, start, end):
        latent = rows_of(win.at[2], [shard[k] for k in sets[i]])

        for g in range(start, end):
            columns = pl.ds(g * 512, 512)
            k_s[pl.ds(T * i, T), columns] = expand(latent, wk_s[:, columns])
            v_s[pl.ds(T * i, T), columns] = expand(latent, wv_s[:, columns])

    def attend(i, first, heads):
        rows = pl.ds(T * i, T)
        tail = tail_s[rows, :]
        for head in range(first, first + heads):
            columns = pl.ds(head * 128, 128)
            keys = jnp.concatenate([k_s[rows, columns], tail], axis=1)
            weights = jnp.exp2(scores(qp[head], keys) + causal_s[i]).astype(BF16)
            part = jnp.dot(weights, with_ones(v_s[rows, columns]), preferred_element_type=F32)
            acc_s[head] = part if i == 0 else acc_s[head] + part

    def to_partner(k):
        return remote(piece(0, k), piece(0, k), send.at[40 + k], recv.at[0, k ^ 1], peers["partner"])

    def earlier_shard(k, pass_on=True):
        pl.when(ctx >= 2)(lambda: got(0, k))
        if pass_on:
            to_partner(k).start()
        relay_if(0, k)

    straight = jnp.logical_not(turn)

    def in_time(k):
        pl.when(straight)(lambda: earlier_shard(k))

    def late(k, pass_on):
        pl.when(turn)(lambda: earlier_shard(k, pass_on))

    def partner_shard():
        got(0, 1)
        relay_if(0, 1)

    query_at = lax.broadcasted_iota(jnp.int32, (512, 64), 0)
    ahead = query_at - lax.broadcasted_iota(jnp.int32, (512, 64), 1)
    for i in range(2):
        visible = jnp.concatenate([jnp.where(ahead >= shard[k] * 64, 0.0, -BIG) for k in sets[i]], axis=1)
        causal_s[i] = visible

    got(1, 1)
    for where in ("right", "left", "far"):
        give(1, 1, where)
    relay_if(1, 1)
    got(1, 2)
    give(1, 2, "next", forward)
    got(1, 4)
    give(1, 4, "next", forward)
    relay_if(1, 2)
    relay_if(1, 4)
    in_time(0)
    loads[3].wait()
    loads[4].wait()
    tails(0)
    widen(0, 0, 4)
    late(0, True)
    for where in ("far", "right", "left"):
        give(0, 0, where, turn)
    attend(0, 0, 8)
    got(1, 6)
    give(1, 6, "next", forward)
    relay_if(1, 6)
    in_time(2)
    attend(0, 8, 8)
    got(1, 3)
    relay_if(1, 3)
    got(1, 5)
    relay_if(1, 5)
    in_time(4)
    got(1, 7)
    relay_if(1, 7)
    pl.when(turn)(partner_shard)
    for where in ("right", "left"):
        give(0, 1, where, turn)
    tails(1)
    widen(1, 0, 2)
    in_time(6)
    widen(1, 2, 4)
    late(2, False)
    late(4, False)
    late(6, True)
    attend(1, 0, 8)
    attend(1, 8, 4)
    pl.when(straight)(partner_shard)
    got(0, 3)
    relay_if(0, 3)
    attend(1, 12, 4)
    for k in (5, 7):
        got(0, k)
        relay_if(0, k)

    pl.when(ctx >= 1)(d1.wait_recv)
    pl.when(ctx >= 2)(d2.wait_recv)
    for k in range(8):
        place = win.at[1, shard[k]]
        remote(place, place, relay_send.at[k], relay_recv.at[k], sibling).wait_recv()
    for c, condition in started:
        if condition is None:
            c.wait_send()
        else:
            pl.when(condition)(c.wait_send)
    for k in (0, 6):
        to_partner(k).wait_send()
    for k in (2, 4):
        pl.when(straight)(to_partner(k).wait_send)
    for k in range(8):
        relay(k).wait_send()
    pl.when(ctx < 14)(d2.wait_send)
    pl.when(ctx < 15)(d1.wait_send)


def gather(latent, docs, queries, w_key, w_value):
    vmem, hbm = pl.BlockSpec(memory_space=pltpu.VMEM), pl.BlockSpec(memory_space=pltpu.HBM)
    operands = [pltpu.with_memory_space_constraint(a, pltpu.HBM) for a in (latent, docs, queries, w_key, w_value)]
    return pl.pallas_call(
        gather_kernel,
        out_shape=(
            pltpu.VMEM((3, 8, 32, 1152), BF16),
            pltpu.VMEM((3, 4, 128), jnp.int32),
            pltpu.VMEM((HEADS, 512, 256), BF16),
            pltpu.VMEM((512, 2048), BF16),
            pltpu.VMEM((512, 2048), BF16),
            pltpu.VMEM((HEADS, 512, 256), F32),
        ),
        in_specs=[hbm] * 5,
        out_specs=(vmem,) * 6,
        scratch_shapes=[
            pltpu.VMEM((64, 576), BF16),
            pltpu.VMEM((32, 1152), BF16),
            pltpu.VMEM((512, 3072), BF16),
            pltpu.VMEM((512, HEADS * 128), BF16),
            pltpu.VMEM((512, HEADS * 128), BF16),
            pltpu.VMEM((512, 128), BF16),
            pltpu.VMEM((512, 128), BF16),
            pltpu.VMEM((512, 128), BF16),
            pltpu.VMEM((2, 512, T), F32),
            pltpu.SemaphoreType.DMA((48,)),
            pltpu.SemaphoreType.DMA((2, 8)),
            pltpu.SemaphoreType.DMA((8,)),
            pltpu.SemaphoreType.DMA((8,)),
            pltpu.SemaphoreType.DMA((2,)),
            pltpu.SemaphoreType.DMA((2,)),
            pltpu.SemaphoreType.DMA((5,)),
        ],
        compiler_params=pltpu.CompilerParams(collective_id=0, has_side_effects=True, vmem_limit_bytes=20 * 2**20),
    )(*operands)


def earlier_kernel(win_ref, docs_ref, qp, wk_ref, wv_ref, acc_ref, out_ref, o_s, k_s, v_s, k2_s, v2_s, tail_s, rng_s, out_sem):
    wide = ((k_s, v_s), (k2_s, v2_s))

    def document(row):
        b, rest = divmod(row, 512)
        return docs_ref[b, rest // 128, rest % 128]

    def first_chunk(block):
        lowest = jnp.int32(4)
        for c in reversed(range(block, 4)):
            lowest = jnp.where(document(c * T + T - 1) == document(1024 + block * T), c, lowest)
        return lowest

    first, both = first_chunk(0), first_chunk(1) < 4
    window = win_ref.reshape(24, 32, 1152)

    def tails(start, end):
        for r in range(start, end):
            rope = rope_of(window, (2 * r, 2 * r + 1))
            tail_s[pl.ds(128 * r, 128), :] = key_tail(rope, document_mask(docs_ref[r // 4, r % 4:r % 4 + 1, :]))

    rng_s[0] = jnp.ones((T, 128), F32)
    rng_s[1] = jnp.ones((T, 128), F32)

    def store(head, row, acc):
        total = acc[:, 128:]
        o_s[head, pl.ds(row, acc.shape[0]), :] = (acc[:, :128] / total).astype(BF16)
        for t in range(acc.shape[0] // T):
            rng_s[0] = jnp.minimum(rng_s[0], total[t * T:(t + 1) * T])
            rng_s[1] = jnp.maximum(rng_s[1], total[t * T:(t + 1) * T])

    def write(head):
        return pltpu.make_async_copy(o_s.at[head], out_ref.at[:, pl.ds(pl.multiple_of(head * 128, 128), 128)], out_sem.at[head])

    def run(start, reach):
        count = 4 - start
        every = pl.ds(0, count * T)

        def widen(head, heads, k, v):
            part = pl.ds(pl.multiple_of(head * 128, 128), heads * 128)
            latent = rows_of(window, range(4 * start, 16))
            k[every, pl.ds(0, heads * 128)] = expand(latent, wk_ref[:, part])
            v[every, pl.ds(0, heads * 128)] = expand(latent, wv_ref[:, part])

        def attend(first_head, heads, k, v):
            for h in range(heads):
                head = first_head + h
                own = slice(h * 128, h * 128 + 128)
                acc = acc_ref[head, pl.ds(0, reach), :]
                for c in range(count):
                    rows = pl.ds(c * T, T)
                    keys = jnp.concatenate([k[rows, own], tail_s[pl.ds((start + c) * T, T), :]], axis=1)
                    weights = jnp.exp2(scores(qp[head, pl.ds(0, reach), :], keys)).astype(BF16)
                    acc = acc + jnp.dot(weights, with_ones(v[rows, own]), preferred_element_type=F32)
                store(head, 0, acc)
                if reach < 512:
                    store(head, reach, acc_ref[head, pl.ds(reach, 512 - reach), :])
                write(head).start()

        if count:
            tails(2 * start, 8)

        if (start, reach) in UNROLLED:
            slots = ((k_s, v_s), (k2_s, v2_s))
            widen(0, SOME, *slots[0])
            for i in range(HEADS // SOME):
                if (i + 1) * SOME < HEADS:
                    widen((i + 1) * SOME, SOME, *slots[(i + 1) % 2])
                attend(i * SOME, SOME, *slots[i % 2])
        else:
            def step(i, carry):
                if count:
                    widen(4 * i, 4, k_s, v_s)
                attend(4 * i, 4, k_s, v_s)
                return carry

            lax.fori_loop(0, HEADS // 4, step, 0)

    for start in range(5):
        for reach in ((512,) if start == 4 else (256,) if start == 0 else (256, 512)):
            chosen = first == start
            if start < 4:
                chosen = chosen & (both if reach == 512 else jnp.logical_not(both))
            pl.when(chosen)(functools.partial(run, start, reach))
    for head in range(HEADS):
        write(head).wait()

    inside = (jnp.min(rng_s[0]) >= LOW) & (jnp.max(rng_s[1]) <= HIGH)

    @pl.when(jnp.logical_not(inside))
    def _():
        tails(0, 12)

        def one(head, carry):
            part = pl.ds(pl.multiple_of(head * 128, 128), 128)
            own = pl.ds(0, 128)

            def widen(c, carry):
                latent = rows_of(window, [4 * c + i for i in range(4)])
                rows = pl.ds(pl.multiple_of(c * T, T), T)
                k_s[rows, own] = expand(latent, wk_ref[:, part])
                v_s[rows, own] = expand(latent, wv_ref[:, part])
                return carry

            lax.fori_loop(first, 6, widen, 0)
            causal = causal_mask()
            for qb in range(2):
                end = 4 + qb

                def body(c, state):
                    peak, acc = state
                    rows = pl.ds(pl.multiple_of(c * T, T), T)
                    keys = jnp.concatenate([k_s[rows, own], tail_s[rows, :]], axis=1)
                    s = scores(qp[head, pl.ds(qb * T, T), :], keys)
                    s = jnp.where(causal | (c < end), s, -BIG)
                    new = jnp.maximum(peak, jnp.max(s, axis=1, keepdims=True))
                    weights = jnp.exp2(s - new).astype(BF16)
                    t = jnp.dot(weights, with_ones(v_s[rows, own]), preferred_element_type=F32)
                    return new, acc * jnp.exp2(peak - new) + t

                initial = (jnp.full((T, 1), -BIG, F32), jnp.zeros((T, 256), F32))
                _, acc = lax.fori_loop(first, end + 1, body, initial)
                o_s[head, pl.ds(qb * T, T), :] = (acc[:, :128] / acc[:, 128:]).astype(BF16)
            write(head).start()
            write(head).wait()
            return carry

        lax.fori_loop(0, HEADS, one, 0)


def earlier(window, docs, qp, w_key, w_value, acc):
    vmem, hbm = pl.BlockSpec(memory_space=pltpu.VMEM), pl.BlockSpec(memory_space=pltpu.HBM)
    return pl.pallas_call(
        earlier_kernel,
        out_shape=jax.ShapeDtypeStruct((512, 2048), BF16),
        in_specs=[vmem] * 6,
        out_specs=hbm,
        scratch_shapes=[
            pltpu.VMEM((HEADS, 512, 128), BF16),
            pltpu.VMEM((1536, 512), BF16),
            pltpu.VMEM((1536, 512), BF16),
            pltpu.VMEM((1024, 512), BF16),
            pltpu.VMEM((1024, 512), BF16),
            pltpu.VMEM((1536, 128), BF16),
            pltpu.VMEM((2, T, 128), F32),
            pltpu.SemaphoreType.DMA((HEADS,)),
        ],
        compiler_params=pltpu.CompilerParams(vmem_limit_bytes=26 * 2**20),
    )(window, docs, qp, w_key, w_value, acc)


def on_device(queries, latent_cache, doc_ids, w_key, w_value):
    window, docs, qp, wk, wv, acc = gather(latent_cache, doc_ids.reshape(4, 128), queries, w_key, w_value)
    return earlier(window, docs, qp, wk, wv, acc)


def solution(mesh):
    placed = (P("ctx", "dp"), P(("ctx", "dp"), None), P("ctx"), P(None, "dp"), P(None, "dp"))
    return jax.shard_map(on_device, mesh=mesh, in_specs=placed, out_specs=P("ctx", "dp"), check_vma=False)
```

```python
import functools
import math

import jax
import jax.numpy as jnp
from jax import lax
from jax.experimental import pallas as pl
from jax.experimental.pallas import tpu as pltpu
from jax.sharding import PartitionSpec as P

MESH = pl.DeviceIdType.MESH
BF16, F32 = jnp.bfloat16, jnp.float32
HEADS = 16
UNROLLED = ((1, 512), (0, 256))
SOME = 2
T = 256
BIG = 1e30
SCALE = math.log2(math.e) / math.sqrt(192)
LOW, HIGH = 2.0 ** -60, 2.0 ** 100
NT = (((1,), (1,)), ((), ()))


def scores(query, keys):
    return lax.dot_general(query, keys, NT, preferred_element_type=F32) * SCALE


def with_ones(value):
    return jnp.concatenate([value, jnp.ones((value.shape[0], 128), BF16)], axis=1)


def expand(rows, weight):
    return jnp.dot(rows, weight, preferred_element_type=F32).astype(BF16)


def documents_down(row):
    return jnp.transpose(jnp.broadcast_to(row, (128, 128)).astype(F32)).astype(jnp.int32)


def document_mask(row):
    lane = lax.broadcasted_iota(jnp.int32, (128, 128), 1)
    other = (lane >= 64) & (lane < 80) & (documents_down(row) != lane - 64)
    return jnp.where(other, -BIG, 0.0).astype(BF16)


def key_tail(rope, mask):
    return jnp.concatenate([rope, mask[:, 64:]], axis=1)


def query_tail(row):
    lane = lax.broadcasted_iota(jnp.int32, (128, 128), 1)
    return (documents_down(row) == lane - 64).astype(F32).astype(BF16)


def causal_mask():
    return lax.broadcasted_iota(jnp.int32, (T, T), 1) <= lax.broadcasted_iota(jnp.int32, (T, T), 0)


def rows_of(window, shards):
    return jnp.concatenate([window[k, :, 512 * j:512 * j + 512] for k in shards for j in range(2)], axis=0)


def rope_of(window, shards):
    packed = [window[k, :, 1024:] for k in shards]
    return jnp.concatenate([p[:, 64 * j:64 * j + 64] for p in packed for j in range(2)], axis=0)


def gather_kernel(lat_ref, docs_ref, q_ref, wk_ref, wv_ref,
                  win, docs_s, qp, wk_s, wv_s, acc_s,
                  lat_s, own_s, q_s, k_s, v_s, tail_s, qtail_s, mask_s, causal_s,
                  send, recv, relay_send, relay_recv, misc_send, misc_recv, load_sem):
    ctx, dp = lax.axis_index("ctx"), lax.axis_index("dp")
    x, y, core = dp // 2, dp % 2, ctx % 2
    right_x, left_x, far_x = (x + 1) % 4, (x + 3) % 4, (x + 2) % 4
    next1, next2 = ((ctx + 1) % 16, dp), ((ctx + 2) % 16, dp)
    prev1, prev2 = ((ctx + 15) % 16, dp), ((ctx + 14) % 16, dp)
    sibling = (ctx + 1 - 2 * core, dp)
    peers = {
        "partner": (ctx, x * 2 + 1 - y), "right": (ctx, right_x * 2 + y), "left": (ctx, left_x * 2 + y),
        "far": (ctx, far_x * 2 + y), "next": next2}
    turn = ctx // 2 == 4
    before_turn = ctx // 2 == 3
    shard = [column * 2 + row for column in (x, left_x, right_x, far_x) for row in (y, 1 - y)]
    kind_there = {
        "partner": lambda k: k ^ 1, "right": lambda k: 2 + k, "left": lambda k: 4 + k, "far": lambda k: 6 + k,
        "next": lambda k: k}

    barrier = pltpu.get_barrier_semaphore()

    def greet(peer):
        pl.semaphore_signal(barrier, inc=1, device_id=peer, device_id_type=MESH)

    for name in ("partner", "right", "left", "far"):
        greet(peers[name])
    pl.when(ctx >= 1)(lambda: greet(prev1))
    pl.when(ctx >= 2)(lambda: greet(prev2))
    pl.when(core == 0)(lambda: greet(sibling))

    loads = [pltpu.make_async_copy(src, dst, load_sem.at[i]) for i, (src, dst) in enumerate((
        (lat_ref, lat_s), (docs_ref, docs_s.at[2]), (q_ref, q_s), (wk_ref, wk_s), (wv_ref, wv_s)))]
    for c in loads:
        c.start()

    def remote(src, dst, send_sem, recv_sem, peer):
        return pltpu.make_async_remote_copy(
            src_ref=src, dst_ref=dst, send_sem=send_sem, recv_sem=recv_sem, device_id=peer, device_id_type=MESH)

    def piece(w, k):
        return win.at[2 * w, shard[k]]

    started = []

    def give(w, k, where, condition=None):
        to = 0 if where == "next" else w
        src = own_s if (w, k) == (1, 0) else piece(w, k)
        c = remote(src, win.at[2 * to, shard[k]], send.at[len(started)], recv.at[to, kind_there[where](k)], peers[where])
        started.append((c, condition))
        if condition is None:
            c.start()
        else:
            pl.when(condition)(c.start)

    def got(w, k):
        remote(piece(w, k), piece(w, k), send.at[0], recv.at[w, k], sibling).wait_recv()

    def relay(k):
        return remote(win.at[2 - 2 * core, shard[k]], win.at[1, shard[k]], relay_send.at[k], relay_recv.at[k], sibling)

    def relay_if(w, k):
        pl.when(core == 1 - w)(lambda: relay(k).start())

    loads[0].wait()
    packed = jnp.concatenate(
        [lat_s[:32, :512], lat_s[32:, :512], lat_s[:32, 512:], lat_s[32:, 512:]], axis=1)
    own_s[...] = packed
    win[2, dp] = packed

    d1 = remote(docs_ref, docs_s.at[1], misc_send.at[0], misc_recv.at[0], next1)
    d2 = remote(docs_ref, docs_s.at[0], misc_send.at[1], misc_recv.at[1], next2)

    forward = (ctx < 14) & jnp.logical_not(before_turn)
    pl.semaphore_wait(barrier, 4 + jnp.where(ctx < 15, 1, 0) + jnp.where(ctx < 14, 1, 0) + core)

    give(1, 0, "next", before_turn)
    for where in ("partner", "right", "left", "far"):
        give(1, 0, where)
    give(1, 0, "next", forward)
    pl.when(ctx < 14)(d2.start)
    pl.when(ctx < 15)(d1.start)
    relay_if(1, 0)

    loads[1].wait()
    for r in range(4):
        qtail_s[pl.ds(128 * r, 128), :] = query_tail(docs_s[2, r:r + 1, :])
        mask_s[pl.ds(128 * r, 128), :] = document_mask(docs_s[2, r:r + 1, :])

    @pl.when(ctx < 2)
    def _():
        docs_s[0] = jnp.full((4, 128), -1, jnp.int32)
        for k in (0, 2, 4, 6):
            win[0, shard[k]] = own_s[...]

    @pl.when(ctx < 1)
    def _():
        docs_s[1] = jnp.full((4, 128), -1, jnp.int32)

    loads[2].wait()
    qtail = qtail_s[...]

    def prepare(p, carry):
        a, b, c = [q_s[:, pl.ds(pl.multiple_of(p * 384 + 128 * i, 128), 128)] for i in range(3)]
        qp[2 * p, :, :128] = a
        qp[2 * p, :, 128:] = jnp.concatenate([b[:, :64], qtail[:, 64:]], axis=1)
        qp[2 * p + 1, :, :128] = jnp.concatenate([b[:, 64:], c[:, :64]], axis=1)
        qp[2 * p + 1, :, 128:] = jnp.concatenate([c[:, 64:], qtail[:, 64:]], axis=1)
        return carry

    lax.fori_loop(0, HEADS // 2, prepare, 0)

    sets = ((0, 1, 2, 4), (3, 5, 6, 7))

    def tails(i):
        rope = rope_of(win.at[2], [shard[k] for k in sets[i]])
        for n, k in enumerate(sets[i]):
            mask = mask_s[pl.ds(pl.multiple_of(shard[k] * 64, 64), 64), :]
            tail_s[pl.ds(T * i + 64 * n, 64), :] = key_tail(rope[64 * n:64 * n + 64], mask)

    def widen(i, start, end):
        latent = rows_of(win.at[2], [shard[k] for k in sets[i]])

        def some(g, carry):
            columns = pl.ds(pl.multiple_of(g * 1024, 1024), 1024)
            k_s[pl.ds(T * i, T), columns] = expand(latent, wk_s[:, columns])
            v_s[pl.ds(T * i, T), columns] = expand(latent, wv_s[:, columns])
            return carry

        lax.fori_loop(start // 2, end // 2, some, 0)

    def attend(i, first, heads):
        rows = pl.ds(T * i, T)
        tail = tail_s[rows, :]
        for head in range(first, first + heads):
            columns = pl.ds(head * 128, 128)
            keys = jnp.concatenate([k_s[rows, columns], tail], axis=1)
            weights = jnp.exp2(scores(qp[head], keys) + causal_s[i]).astype(BF16)
            part = jnp.dot(weights, with_ones(v_s[rows, columns]), preferred_element_type=F32)
            acc_s[head] = part if i == 0 else acc_s[head] + part

    def to_partner(k):
        return remote(piece(0, k), piece(0, k), send.at[40 + k], recv.at[0, k ^ 1], peers["partner"])

    def earlier_shard(k, pass_on=True):
        pl.when(ctx >= 2)(lambda: got(0, k))
        if pass_on:
            to_partner(k).start()
        relay_if(0, k)

    straight = jnp.logical_not(turn)

    def in_time(k):
        pl.when(straight)(lambda: earlier_shard(k))

    def late(k, pass_on):
        pl.when(turn)(lambda: earlier_shard(k, pass_on))

    def partner_shard():
        got(0, 1)
        relay_if(0, 1)

    query_at = lax.broadcasted_iota(jnp.int32, (512, 64), 0)
    ahead = query_at - lax.broadcasted_iota(jnp.int32, (512, 64), 1)
    for i in range(2):
        visible = jnp.concatenate([jnp.where(ahead >= shard[k] * 64, 0.0, -BIG) for k in sets[i]], axis=1)
        causal_s[i] = visible

    got(1, 1)
    for where in ("right", "left", "far"):
        give(1, 1, where)
    relay_if(1, 1)
    got(1, 2)
    give(1, 2, "next", forward)
    got(1, 4)
    give(1, 4, "next", forward)
    relay_if(1, 2)
    relay_if(1, 4)
    in_time(0)
    loads[3].wait()
    loads[4].wait()
    tails(0)
    widen(0, 0, 4)
    late(0, True)
    for where in ("far", "right", "left"):
        give(0, 0, where, turn)
    attend(0, 0, 8)
    got(1, 6)
    give(1, 6, "next", forward)
    relay_if(1, 6)
    in_time(2)
    attend(0, 8, 8)
    got(1, 3)
    relay_if(1, 3)
    got(1, 5)
    relay_if(1, 5)
    in_time(4)
    got(1, 7)
    relay_if(1, 7)
    pl.when(turn)(partner_shard)
    for where in ("right", "left"):
        give(0, 1, where, turn)
    tails(1)
    widen(1, 0, 2)
    in_time(6)
    widen(1, 2, 4)
    late(2, False)
    late(4, False)
    late(6, True)
    attend(1, 0, 8)
    attend(1, 8, 4)
    pl.when(straight)(partner_shard)
    got(0, 3)
    relay_if(0, 3)
    attend(1, 12, 4)
    for k in (5, 7):
        got(0, k)
        relay_if(0, k)

    pl.when(ctx >= 1)(d1.wait_recv)
    pl.when(ctx >= 2)(d2.wait_recv)
    for k in range(8):
        place = win.at[1, shard[k]]
        remote(place, place, relay_send.at[k], relay_recv.at[k], sibling).wait_recv()
    for c, condition in started:
        if condition is None:
            c.wait_send()
        else:
            pl.when(condition)(c.wait_send)
    for k in (0, 6):
        to_partner(k).wait_send()
    for k in (2, 4):
        pl.when(straight)(to_partner(k).wait_send)
    for k in range(8):
        relay(k).wait_send()
    pl.when(ctx < 14)(d2.wait_send)
    pl.when(ctx < 15)(d1.wait_send)


def gather(latent, docs, queries, w_key, w_value):
    vmem, hbm = pl.BlockSpec(memory_space=pltpu.VMEM), pl.BlockSpec(memory_space=pltpu.HBM)
    operands = [pltpu.with_memory_space_constraint(a, pltpu.HBM) for a in (latent, docs, queries, w_key, w_value)]
    return pl.pallas_call(
        gather_kernel,
        out_shape=(
            pltpu.VMEM((3, 8, 32, 1152), BF16),
            pltpu.VMEM((3, 4, 128), jnp.int32),
            pltpu.VMEM((HEADS, 512, 256), BF16),
            pltpu.VMEM((512, 2048), BF16),
            pltpu.VMEM((512, 2048), BF16),
            pltpu.VMEM((HEADS, 512, 256), F32),
        ),
        in_specs=[hbm] * 5,
        out_specs=(vmem,) * 6,
        scratch_shapes=[
            pltpu.VMEM((64, 576), BF16),
            pltpu.VMEM((32, 1152), BF16),
            pltpu.VMEM((512, 3072), BF16),
            pltpu.VMEM((512, HEADS * 128), BF16),
            pltpu.VMEM((512, HEADS * 128), BF16),
            pltpu.VMEM((512, 128), BF16),
            pltpu.VMEM((512, 128), BF16),
            pltpu.VMEM((512, 128), BF16),
            pltpu.VMEM((2, 512, T), F32),
            pltpu.SemaphoreType.DMA((48,)),
            pltpu.SemaphoreType.DMA((2, 8)),
            pltpu.SemaphoreType.DMA((8,)),
            pltpu.SemaphoreType.DMA((8,)),
            pltpu.SemaphoreType.DMA((2,)),
            pltpu.SemaphoreType.DMA((2,)),
            pltpu.SemaphoreType.DMA((5,)),
        ],
        compiler_params=pltpu.CompilerParams(collective_id=0, has_side_effects=True, vmem_limit_bytes=20 * 2**20),
    )(*operands)


def earlier_kernel(win_ref, docs_ref, qp, wk_ref, wv_ref, acc_ref, out_ref, o_s, k_s, v_s, k2_s, v2_s, tail_s, rng_s, out_sem):
    wide = ((k_s, v_s), (k2_s, v2_s))

    def document(row):
        b, rest = divmod(row, 512)
        return docs_ref[b, rest // 128, rest % 128]

    def first_chunk(block):
        lowest = jnp.int32(4)
        for c in reversed(range(block, 4)):
            lowest = jnp.where(document(c * T + T - 1) == document(1024 + block * T), c, lowest)
        return lowest

    first, both = first_chunk(0), first_chunk(1) < 4
    window = win_ref.reshape(24, 32, 1152)

    def tails(start, end):
        for r in range(start, end):
            rope = rope_of(window, (2 * r, 2 * r + 1))
            tail_s[pl.ds(128 * r, 128), :] = key_tail(rope, document_mask(docs_ref[r // 4, r % 4:r % 4 + 1, :]))

    rng_s[0] = jnp.ones((T, 128), F32)
    rng_s[1] = jnp.ones((T, 128), F32)

    def store(head, row, acc):
        total = acc[:, 128:]
        o_s[head, pl.ds(row, acc.shape[0]), :] = (acc[:, :128] / total).astype(BF16)
        for t in range(acc.shape[0] // T):
            rng_s[0] = jnp.minimum(rng_s[0], total[t * T:(t + 1) * T])
            rng_s[1] = jnp.maximum(rng_s[1], total[t * T:(t + 1) * T])

    def write(head):
        return pltpu.make_async_copy(o_s.at[head], out_ref.at[:, pl.ds(pl.multiple_of(head * 128, 128), 128)], out_sem.at[head])

    def run(start, reach):
        count = 4 - start
        every = pl.ds(0, count * T)

        def widen(head, heads, k, v):
            part = pl.ds(pl.multiple_of(head * 128, 128), heads * 128)
            latent = rows_of(window, range(4 * start, 16))
            k[every, pl.ds(0, heads * 128)] = expand(latent, wk_ref[:, part])
            v[every, pl.ds(0, heads * 128)] = expand(latent, wv_ref[:, part])

        def attend(first_head, heads, k, v):
            for h in range(heads):
                head = first_head + h
                own = slice(h * 128, h * 128 + 128)
                acc = acc_ref[head, pl.ds(0, reach), :]
                for c in range(count):
                    rows = pl.ds(c * T, T)
                    keys = jnp.concatenate([k[rows, own], tail_s[pl.ds((start + c) * T, T), :]], axis=1)
                    weights = jnp.exp2(scores(qp[head, pl.ds(0, reach), :], keys)).astype(BF16)
                    acc = acc + jnp.dot(weights, with_ones(v[rows, own]), preferred_element_type=F32)
                store(head, 0, acc)
                if reach < 512:
                    store(head, reach, acc_ref[head, pl.ds(reach, 512 - reach), :])
                write(head).start()

        if count:
            tails(2 * start, 8)

        if (start, reach) in UNROLLED:
            slots = ((k_s, v_s), (k2_s, v2_s))
            widen(0, SOME, *slots[0])
            for i in range(HEADS // SOME):
                if (i + 1) * SOME < HEADS:
                    widen((i + 1) * SOME, SOME, *slots[(i + 1) % 2])
                attend(i * SOME, SOME, *slots[i % 2])
        else:
            heads = 4 if (start, reach) in ((2, 512), (1, 256)) else 2

            def step(i, carry):
                if count:
                    widen(heads * i, heads, k_s, v_s)
                attend(heads * i, heads, k_s, v_s)
                return carry

            lax.fori_loop(0, HEADS // heads, step, 0)

    for start in range(5):
        for reach in ((512,) if start == 4 else (256,) if start == 0 else (256, 512)):
            chosen = first == start
            if start < 4:
                chosen = chosen & (both if reach == 512 else jnp.logical_not(both))
            pl.when(chosen)(functools.partial(run, start, reach))
    for head in range(HEADS):
        write(head).wait()

    inside = (jnp.min(rng_s[0]) >= LOW) & (jnp.max(rng_s[1]) <= HIGH)

    @pl.when(jnp.logical_not(inside))
    def _():
        tails(0, 12)

        def one(head, carry):
            part = pl.ds(pl.multiple_of(head * 128, 128), 128)
            own = pl.ds(0, 128)

            def widen(c, carry):
                latent = rows_of(window, [4 * c + i for i in range(4)])
                rows = pl.ds(pl.multiple_of(c * T, T), T)
                k_s[rows, own] = expand(latent, wk_ref[:, part])
                v_s[rows, own] = expand(latent, wv_ref[:, part])
                return carry

            lax.fori_loop(first, 6, widen, 0)
            causal = causal_mask()
            for qb in range(2):
                end = 4 + qb

                def body(c, state):
                    peak, acc = state
                    rows = pl.ds(pl.multiple_of(c * T, T), T)
                    keys = jnp.concatenate([k_s[rows, own], tail_s[rows, :]], axis=1)
                    s = scores(qp[head, pl.ds(qb * T, T), :], keys)
                    s = jnp.where(causal | (c < end), s, -BIG)
                    new = jnp.maximum(peak, jnp.max(s, axis=1, keepdims=True))
                    weights = jnp.exp2(s - new).astype(BF16)
                    t = jnp.dot(weights, with_ones(v_s[rows, own]), preferred_element_type=F32)
                    return new, acc * jnp.exp2(peak - new) + t

                initial = (jnp.full((T, 1), -BIG, F32), jnp.zeros((T, 256), F32))
                _, acc = lax.fori_loop(first, end + 1, body, initial)
                o_s[head, pl.ds(qb * T, T), :] = (acc[:, :128] / acc[:, 128:]).astype(BF16)
            write(head).start()
            write(head).wait()
            return carry

        lax.fori_loop(0, HEADS, one, 0)


def earlier(window, docs, qp, w_key, w_value, acc):
    vmem, hbm = pl.BlockSpec(memory_space=pltpu.VMEM), pl.BlockSpec(memory_space=pltpu.HBM)
    return pl.pallas_call(
        earlier_kernel,
        out_shape=jax.ShapeDtypeStruct((512, 2048), BF16),
        in_specs=[vmem] * 6,
        out_specs=hbm,
        scratch_shapes=[
            pltpu.VMEM((HEADS, 512, 128), BF16),
            pltpu.VMEM((1536, 512), BF16),
            pltpu.VMEM((1536, 512), BF16),
            pltpu.VMEM((1024, 512), BF16),
            pltpu.VMEM((1024, 512), BF16),
            pltpu.VMEM((1536, 128), BF16),
            pltpu.VMEM((2, T, 128), F32),
            pltpu.SemaphoreType.DMA((HEADS,)),
        ],
        compiler_params=pltpu.CompilerParams(vmem_limit_bytes=26 * 2**20),
    )(window, docs, qp, w_key, w_value, acc)


def on_device(queries, latent_cache, doc_ids, w_key, w_value):
    window, docs, qp, wk, wv, acc = gather(latent_cache, doc_ids.reshape(4, 128), queries, w_key, w_value)
    return earlier(window, docs, qp, wk, wv, acc)


def solution(mesh):
    placed = (P("ctx", "dp"), P(("ctx", "dp"), None), P("ctx"), P(None, "dp"), P(None, "dp"))
    return jax.shard_map(on_device, mesh=mesh, in_specs=placed, out_specs=P("ctx", "dp"), check_vma=False)
```
